32 devices in a mesh: sp: 8 (over z, y), dp: 4 (over x, core).
Axes of the slice: x: 2, y: 2, z: 4, core: 2. Of those that a mesh axis runs over, the one named last changes fastest.
Arguments:
- queries: bfloat16 [4096, 8192], P(('dp', 'sp')), parts along dimension 0, may hold values from -60 to 60
- key_heads: bfloat16 [4096, 1024], P(('dp', 'sp')), parts along dimension 0, may hold values from -6 to 6
- value_heads: bfloat16 [4096, 1024], P(('dp', 'sp')), parts along dimension 0, may hold values from -6 to 6
- out_grad: bfloat16 [4096, 8192], P(('dp', 'sp')), parts along dimension 0, may hold values from -6 to 6
- segment_ids: int32 [4096], P(('dp', 'sp')), parts along dimension 0, may hold values from 0 to 3, never falling along the last dimension, each value on 1 to 512 neighbouring positions
Outputs:
- d_query: bfloat16 [4096, 8192], P(('dp', 'sp')), parts along dimension 0
- d_key: bfloat16 [4096, 1024], P(('dp', 'sp')), parts along dimension 0
- d_value: bfloat16 [4096, 1024], P(('dp', 'sp')), parts along dimension 0
The draws below stay inside these ranges and needn't reach their ends.
There are 4 independent parts, one for each index of `dp`. The reference program is written for one: setup_inputs(seed, part) draws one part's arguments, and reference() takes and returns one part's arrays. A program takes and returns all parts, laid end to end along the dimension named above; each array names one. Nothing has to cross between parts.
Inputs may be any that keep to these rules, and one draw needn't show every extreme that they name: `segment_ids`: documents are runs of consecutive tokens with rising ids, each of at most 512 tokens; one has exactly 512.
All inputs are finite; a program needn't handle non-finite values.
Results may differ from the reference program's by a relative error of at most 0.0065.
Values may be sent and summed in bfloat16 or wider, within the bound.
A program may use at most 192 MiB of HBM per device.

```python
import math
import jax
import jax.numpy as jnp
import numpy as np
from jax import lax

HEADS = 64
KV_HEADS = 8
HEAD_DIM = 128
GROUP = 8
MOST = 512
SEQ = 1024
DOCS = 4


def paired_keys(key):
    raw = jax.random.truncated_normal(key, -4.0, 4.0, (SEQ // 2, 2, KV_HEADS * HEAD_DIM), jnp.float32)
    partner = raw[:, 0]
    return jnp.stack([partner, raw[:, 1]], axis=1).reshape(SEQ, KV_HEADS * HEAD_DIM)


def draw_key_heads(key, part):
    shared = paired_keys(key)
    return shared.astype(jnp.bfloat16)


def draw_queries(key, part):
    key = jax.random.fold_in(key, 3)
    drawn = jax.random.truncated_normal(key, -4.0, 4.0, (SEQ, KV_HEADS, GROUP, HEAD_DIM), jnp.float32)
    return drawn.reshape(SEQ, HEADS * HEAD_DIM).astype(jnp.bfloat16)


def level_of(stream_key, shape, shards, smallest, top_value):
    def one(axis_at, parts):
        draws = jax.random.uniform(jax.random.fold_in(jax.random.fold_in(stream_key, 6), axis_at), (parts,), jnp.float32, smallest / len(shards), top_value / len(shards))
        return jnp.repeat(jnp.exp(draws), shape[axis_at] // parts).reshape((-1,) + (1,) * (len(shape) - axis_at - 1))

    loudness = one(*shards[0])
    for cut in shards[1:]:
        loudness = loudness * one(*cut)
    return loudness


def profile(number_of, total, most, lean):
    portions = [(1 << 20) // math.isqrt(grade ** lean) + 1 for grade in range(2, number_of + 1)]
    rest, given = total - most - (number_of - 1), [1] * (number_of - 1)
    while rest > 0:
        free = [i for i in range(number_of - 1) if given[i] < most]
        whole, left = sum([portions[i] for i in free]), rest
        for i in free:
            more = min(most - given[i], max(1, left * portions[i] // whole), rest)
            given[i] = given[i] + more
            rest = rest - more
    return np.array([most] + given)


def ragged_sizes(own_key, number_of, total, reach, lean):
    if number_of == 2:
        one = jax.random.randint(own_key, (), max(1, total - reach), min(reach, total - 1) + 1)
        return jnp.stack([one, total - one])
    lengths = jnp.asarray(profile(number_of, total, reach, lean), jnp.int32)
    twos = (number_of - 1) // 2
    source_of, receiver = lengths[1:1 + 2 * twos:2], lengths[2:2 + 2 * twos:2]
    slack = jnp.minimum(source_of - 1, reach - receiver)
    shifted = jax.random.randint(jax.random.fold_in(own_key, 1), (twos,), 0, 1 << 20) % (slack + 1)
    lengths = lengths.at[1:1 + 2 * twos:2].set(source_of - shifted).at[2:2 + 2 * twos:2].set(receiver + shifted)
    return lengths[jax.random.permutation(jax.random.fold_in(own_key, 2), number_of)]


def bell_draw(stream_key, dims, spread, most, pieces=(), kind=jnp.bfloat16):
    array = spread * jax.random.normal(stream_key, dims, jnp.float32)
    if pieces:
        array = array * level_of(stream_key, dims, pieces, -0.22, 0.18)
    return jnp.clip(array, -most, most).astype(kind)


def setup_inputs(seed: int = 0, part: int = 0) -> dict:
    key_list = jax.random.split(jax.random.key(seed), 6)
    part_keys = jax.random.split(jax.random.fold_in(key_list[5], part), 6)
    queries = draw_queries(jax.random.fold_in(jax.random.fold_in(key_list[5], part), 71), part)
    key_heads = draw_key_heads(jax.random.fold_in(jax.random.fold_in(key_list[5], part), 71), part)
    value_heads = bell_draw(part_keys[2], (SEQ, KV_HEADS * HEAD_DIM), 1.0, 6.0, ((0, 8),))
    out_grad = bell_draw(part_keys[3], (SEQ, HEADS * HEAD_DIM), 1.0, 6.0, ((0, 8),))
    segment_ids = jnp.searchsorted(jnp.cumsum(ragged_sizes(part_keys[4], DOCS, SEQ, MOST, 2)), jnp.arange(SEQ), side="right").astype(jnp.int32)
    return {"queries": queries, "key_heads": key_heads, "value_heads": value_heads, "out_grad": out_grad, "segment_ids": segment_ids}


def reference(queries, key_heads, value_heads, out_grad, segment_ids):
    scale = HEAD_DIM ** -0.5
    block = min(512, SEQ)
    span = MOST + block
    count = SEQ // block
    kv_width = KV_HEADS * HEAD_DIM
    keys_pad = jnp.concatenate([jnp.zeros((MOST, kv_width), jnp.bfloat16), key_heads], axis=0)
    values_pad = jnp.concatenate([jnp.zeros((MOST, kv_width), jnp.bfloat16), value_heads], axis=0)
    ids_pad = jnp.concatenate([jnp.full((MOST,), -1, jnp.int32), segment_ids.astype(jnp.int32)], axis=0)

    def one_block(carry, number):
        key_acc, value_acc = carry
        start = (number * block).astype(jnp.int32)
        q_blk = lax.dynamic_slice_in_dim(queries, start, block, 0).reshape(block, KV_HEADS, GROUP, HEAD_DIM).astype(jnp.float32)
        g_blk = lax.dynamic_slice_in_dim(out_grad, start, block, 0).reshape(block, KV_HEADS, GROUP, HEAD_DIM).astype(jnp.float32)
        k_win = lax.dynamic_slice_in_dim(keys_pad, start, span, 0).reshape(span, KV_HEADS, HEAD_DIM).astype(jnp.float32)
        v_win = lax.dynamic_slice_in_dim(values_pad, start, span, 0).reshape(span, KV_HEADS, HEAD_DIM).astype(jnp.float32)
        ids_q = lax.dynamic_slice_in_dim(segment_ids.astype(jnp.int32), start, block, 0)
        ids_k = lax.dynamic_slice_in_dim(ids_pad, start, span, 0)
        q_pos = start + jnp.arange(block, dtype=jnp.int32)
        k_pos = start - MOST + jnp.arange(span, dtype=jnp.int32)
        allowed = (ids_q[:, None] == ids_k[None, :]) & (k_pos[None, :] <= q_pos[:, None])
        scores = jnp.einsum("qkgd,jkd->kgqj", q_blk, k_win) * scale
        scores = jnp.where(allowed, scores, -1e30)
        row_max = jnp.max(scores, axis=-1, keepdims=True)
        probs = jnp.exp(scores - row_max)
        probs = probs / jnp.sum(probs, axis=-1, keepdims=True)
        probs_low = lax.optimization_barrier(probs.astype(jnp.bfloat16)).astype(jnp.float32)
        prob_grads = jnp.einsum("qkgd,jkd->kgqj", g_blk, v_win)
        delta = jnp.sum(probs * prob_grads, axis=-1, keepdims=True)
        score_grads = lax.optimization_barrier((probs * (prob_grads - delta)).astype(jnp.bfloat16)).astype(jnp.float32)
        query_grad = jnp.einsum("kgqj,jkd->qkgd", score_grads, k_win) * scale
        key_part = jnp.einsum("kgqj,qkgd->jkd", score_grads, q_blk) * scale
        value_part = jnp.einsum("kgqj,qkgd->jkd", probs_low, g_blk)
        old_key = lax.dynamic_slice_in_dim(key_acc, start, span, 0)
        old_value = lax.dynamic_slice_in_dim(value_acc, start, span, 0)
        key_acc = lax.dynamic_update_slice_in_dim(key_acc, old_key + key_part, start, 0)
        value_acc = lax.dynamic_update_slice_in_dim(value_acc, old_value + value_part, start, 0)
        return (key_acc, value_acc), query_grad.reshape(block, HEADS * HEAD_DIM).astype(jnp.bfloat16)

    zeros_acc = jnp.zeros((SEQ + MOST, KV_HEADS, HEAD_DIM), jnp.float32)
    (key_acc, value_acc), query_blocks = lax.scan(one_block, (zeros_acc, zeros_acc), jnp.arange(count, dtype=jnp.int32))
    d_query = query_blocks.reshape(SEQ, HEADS * HEAD_DIM)
    d_key = key_acc[MOST:].reshape(SEQ, kv_width).astype(jnp.bfloat16)
    d_value = value_acc[MOST:].reshape(SEQ, kv_width).astype(jnp.bfloat16)
    return (d_query, d_key, d_value)
```

```python
import functools

import jax
import jax.numpy as jnp
from jax import lax
from jax.experimental import pallas as pl
from jax.experimental.pallas import tpu as pltpu
from jax.sharding import PartitionSpec as P

HEAD_DIM = 128
MOST = 512
REACH = 4
SLOTS = REACH + 1
LOG2E = 1.4426950408889634
NT = (((1,), (1,)), ((), ()))


def kernel(
    n, kv_count, group,
    q_ref, k_ref, v_ref, g_ref, ids_ref,
    dq_ref, dk_ref, dv_ref,
    kv, ids, bias, probs, grads, part, out_buf, in_buf,
    kv_send, kv_recv, back_send, back_recv, ids_send, ids_recv,
):
    me = lax.axis_index("sp")
    odd = lax.rem(me, 2) == 1
    tokens = q_ref.shape[0]
    span = SLOTS * tokens
    scale = HEAD_DIM ** (-0.5)
    up = me + 2 < n
    partner = jnp.where(odd, me - 1, me + 1)

    def kv_copy(c, src, dst, which, target):
        return pltpu.make_async_remote_copy(
            src_ref=kv.at[c, src],
            dst_ref=kv.at[c, dst],
            send_sem=kv_send.at[c, which],
            recv_sem=kv_recv.at[c, dst - 1],
            device_id={"sp": target},
            device_id_type=pl.DeviceIdType.MESH,
        )

    def back_copy(c, slot, target):
        return pltpu.make_async_remote_copy(
            src_ref=out_buf.at[c, slot - 1],
            dst_ref=in_buf.at[c, slot - 1],
            send_sem=back_send.at[c, slot - 1],
            recv_sem=back_recv.at[c, slot - 1],
            device_id={"sp": target},
            device_id_type=pl.DeviceIdType.MESH,
        )

    def ids_copy(d):
        return pltpu.make_async_remote_copy(
            src_ref=ids_ref,
            dst_ref=ids.at[d],
            send_sem=ids_send.at[d - 1],
            recv_sem=ids_recv.at[d - 1],
            device_id={"sp": me + d},
            device_id_type=pl.DeviceIdType.MESH,
        )

    barrier = pltpu.get_barrier_semaphore()
    for d in range(1, SLOTS):
        @pl.when(me >= d)
        def _():
            pl.semaphore_signal(
                barrier, inc=1, device_id={"sp": me - d}, device_id_type=pl.DeviceIdType.MESH
            )

        @pl.when(me + d < n)
        def _():
            pl.semaphore_signal(
                barrier, inc=1, device_id={"sp": me + d}, device_id_type=pl.DeviceIdType.MESH
            )

    def fill(c, _):
        cols = pl.ds(pl.multiple_of(c * HEAD_DIM, HEAD_DIM), HEAD_DIM)
        kv[c, 0, 0] = k_ref[:, cols]
        kv[c, 0, 1] = v_ref[:, cols]
        for d in range(1, SLOTS):
            @pl.when(me < d)
            def _():
                kv[c, d] = jnp.zeros((2, tokens, HEAD_DIM), kv.dtype)
        return 0

    lax.fori_loop(0, kv_count, fill, 0)
    ids[0] = ids_ref[...]
    for d in range(1, SLOTS):
        @pl.when(me < d)
        def _():
            ids[d] = jnp.full(ids_ref.shape, -1, jnp.int32)

    pl.semaphore_wait(barrier, jnp.minimum(me, REACH) + jnp.minimum(n - 1 - me, REACH))

    def send_own(c):
        @pl.when(up)
        def _():
            kv_copy(c, 0, 2, 0, me + 2).start()

        @pl.when(jnp.logical_not(odd))
        def _():
            kv_copy(c, 0, 1, 2, me + 1).start()

    for d in range(1, SLOTS):
        @pl.when(me + d < n)
        def _():
            ids_copy(d).start()

    ahead = min(2, kv_count)
    for c in range(ahead):
        send_own(c)

    for d in range(1, SLOTS):
        @pl.when(me >= d)
        def _():
            ids_copy(d).wait_recv()

    row = jnp.broadcast_to(ids[0, 0:1, :].astype(jnp.float32), (tokens, tokens))
    for d in range(SLOTS):
        col = jnp.broadcast_to(ids[d, 0:1, :].astype(jnp.float32), (tokens, tokens)).T
        same = col == row
        if d == 0:
            key_at = lax.broadcasted_iota(jnp.int32, (tokens, tokens), 0)
            query_at = lax.broadcasted_iota(jnp.int32, (tokens, tokens), 1)
            same = same & (key_at <= query_at)
        bias[d * tokens:(d + 1) * tokens, :] = jnp.where(same, 0.0, -1e30)

    def stack(ref, c, first, count):
        cols = [
            ref[:, pl.ds(pl.multiple_of((c * group + first + i) * HEAD_DIM, HEAD_DIM), HEAD_DIM)]
            for i in range(count)
        ]
        return jnp.concatenate(cols, axis=0)

    def compute(c):
        keys = kv[c, :, 0].reshape(span, HEAD_DIM)
        values = kv[c, :, 1].reshape(span, HEAD_DIM)
        for pair in range(group // 2):
            q_pair = stack(q_ref, c, 2 * pair, 2)
            g_pair = stack(g_ref, c, 2 * pair, 2)
            blocked = bias[...]
            s = lax.dot_general(keys, q_pair, NT, preferred_element_type=jnp.float32)
            s = s + jnp.concatenate([blocked, blocked], axis=1)
            top = jnp.max(s, axis=0, keepdims=True)
            e = jnp.exp2((s - top) * (scale * LOG2E))
            p = e * (1.0 / jnp.sum(e, axis=0, keepdims=True))
            dp = lax.dot_general(values, g_pair, NT, preferred_element_type=jnp.float32)
            delta = jnp.sum(p * dp, axis=0, keepdims=True)
            lanes = slice(pair * 2 * tokens, (pair + 1) * 2 * tokens)
            probs[:, lanes] = p.astype(jnp.bfloat16)
            grads[:, lanes] = (p * (dp - delta)).astype(jnp.bfloat16)
        dv = jnp.dot(probs[...], stack(g_ref, c, 0, group), preferred_element_type=jnp.float32)
        dk = scale * jnp.dot(
            grads[...], stack(q_ref, c, 0, group), preferred_element_type=jnp.float32
        )
        for d in range(SLOTS):
            for which, array in ((0, dk), (1, dv)):
                block = array[d * tokens:(d + 1) * tokens]
                if d <= 2:
                    part[c, d, which] = block
                else:
                    out_buf[c, d - 1, which] = block.astype(jnp.bfloat16)
        @pl.when(me >= 3)
        def _():
            back_copy(c, 3, me - 2).start()

        @pl.when(me >= 4)
        def _():
            back_copy(c, 4, me - 2).start()

        dq_t = scale * jnp.dot(keys.T, grads[...], preferred_element_type=jnp.float32)
        for h in range(group):
            cols = pl.ds(pl.multiple_of((c * group + h) * HEAD_DIM, HEAD_DIM), HEAD_DIM)
            dq_ref[:, cols] = dq_t[:, h * tokens:(h + 1) * tokens].T.astype(jnp.bfloat16)

    def step(t, _):
        @pl.when(t < kv_count)
        def _():
            @pl.when(t + ahead < kv_count)
            def _():
                send_own(t + ahead)

            @pl.when(me >= 2)
            def _():
                kv_copy(t, 0, 2, 0, me).wait_recv()

                @pl.when(up)
                def _():
                    kv_copy(t, 2, 4, 1, me + 2).start()

                @pl.when(odd)
                def _():
                    kv_copy(t, 2, 1, 2, me - 1).start()

        @pl.when((t >= 1) & (t - 1 < kv_count))
        def _():
            @pl.when(me >= 1)
            def _():
                kv_copy(t - 1, 0, 1, 2, me).wait_recv()

                @pl.when(up)
                def _():
                    kv_copy(t - 1, 1, 3, 3, me + 2).start()

        @pl.when((t >= 2) & (t - 2 < kv_count))
        def _():
            @pl.when(me >= 3)
            def _():
                kv_copy(t - 2, 1, 3, 3, me).wait_recv()

            @pl.when(me >= 4)
            def _():
                kv_copy(t - 2, 2, 4, 1, me).wait_recv()

            compute(t - 2)

        @pl.when((t >= 3) & (t - 3 < kv_count))
        def _():
            c = t - 3

            @pl.when(up & (me >= 1))
            def _():
                back_copy(c, 3, me).wait_recv()
                part[c, 1] += in_buf[c, 2].astype(jnp.float32)

            @pl.when(up & (me >= 2))
            def _():
                back_copy(c, 4, me).wait_recv()
                part[c, 2] += in_buf[c, 3].astype(jnp.float32)

            @pl.when(me >= 1)
            def _():
                out_buf[c, 0] = part[c, 1].astype(jnp.bfloat16)
                back_copy(c, 1, partner).start()

        @pl.when((t >= 4) & (t - 4 < kv_count))
        def _():
            c = t - 4

            @pl.when(odd & (me >= 3))
            def _():
                back_copy(c, 1, me).wait_recv()
                part[c, 2] += in_buf[c, 0].astype(jnp.float32)

            @pl.when(jnp.logical_not(odd))
            def _():
                back_copy(c, 1, me).wait_recv()
                part[c, 0] += in_buf[c, 0].astype(jnp.float32)

            @pl.when(me >= 2)
            def _():
                out_buf[c, 1] = part[c, 2].astype(jnp.bfloat16)
                back_copy(c, 2, me - 2).start()

        @pl.when(t >= 5)
        def _():
            c = t - 5

            @pl.when(up)
            def _():
                back_copy(c, 2, me).wait_recv()
                part[c, 0] += in_buf[c, 1].astype(jnp.float32)

            cols = pl.ds(pl.multiple_of(c * HEAD_DIM, HEAD_DIM), HEAD_DIM)
            dk_ref[:, cols] = part[c, 0, 0].astype(jnp.bfloat16)
            dv_ref[:, cols] = part[c, 0, 1].astype(jnp.bfloat16)

        return 0

    lax.fori_loop(0, kv_count + 5, step, 0)

    def drain(c, _):
        @pl.when(up)
        def _():
            kv_copy(c, 0, 2, 0, me).wait_send()

            @pl.when(me >= 2)
            def _():
                kv_copy(c, 2, 4, 1, me).wait_send()

            @pl.when(me >= 1)
            def _():
                kv_copy(c, 1, 3, 3, me).wait_send()

        @pl.when(jnp.logical_not(odd) | (me >= 3))
        def _():
            kv_copy(c, 0, 1, 2, me).wait_send()

        for slot in range(1, SLOTS):
            @pl.when(me >= slot)
            def _():
                back_copy(c, slot, me).wait_send()
        return 0

    lax.fori_loop(0, kv_count, drain, 0)
    for d in range(1, SLOTS):
        @pl.when(me + d < n)
        def _():
            ids_copy(d).wait_send()


def body(queries, key_heads, value_heads, out_grad, segment_ids):
    tokens, width = queries.shape
    kv_width = key_heads.shape[1]
    kv_count = kv_width // HEAD_DIM
    group = width // kv_width
    n = lax.axis_size("sp")
    assert -(-(MOST - 1) // tokens) == REACH and n % 2 == 0 and group % 2 == 0
    ids_rows = jnp.broadcast_to(segment_ids[None, :], (8, tokens))
    span = SLOTS * tokens
    vmem = pl.BlockSpec(memory_space=pltpu.VMEM)
    pairs = (kv_count, REACH, 2, tokens, HEAD_DIM)
    dma = pltpu.SemaphoreType.DMA
    elements = kv_count * group * tokens * span
    return pl.pallas_call(
        functools.partial(kernel, n, kv_count, group),
        out_shape=(
            jax.ShapeDtypeStruct((tokens, width), jnp.bfloat16),
            jax.ShapeDtypeStruct((tokens, kv_width), jnp.bfloat16),
            jax.ShapeDtypeStruct((tokens, kv_width), jnp.bfloat16),
        ),
        in_specs=[vmem] * 5,
        out_specs=(vmem, vmem, vmem),
        scratch_shapes=[
            pltpu.VMEM((kv_count, SLOTS, 2, tokens, HEAD_DIM), jnp.bfloat16),
            pltpu.VMEM((SLOTS, 8, tokens), jnp.int32),
            pltpu.VMEM((span, tokens), jnp.float32),
            pltpu.VMEM((span, group * tokens), jnp.bfloat16),
            pltpu.VMEM((span, group * tokens), jnp.bfloat16),
            pltpu.VMEM((kv_count, 3, 2, tokens, HEAD_DIM), jnp.float32),
            pltpu.VMEM(pairs, jnp.bfloat16),
            pltpu.VMEM(pairs, jnp.bfloat16),
            dma((kv_count, 4)),
            dma((kv_count, REACH)),
            dma((kv_count, REACH)),
            dma((kv_count, REACH)),
            dma((REACH,)),
            dma((REACH,)),
        ],
        compiler_params=pltpu.CompilerParams(
            collective_id=0, has_side_effects=True, vmem_limit_bytes=48 * 1024 * 1024
        ),
        cost_estimate=pl.CostEstimate(
            flops=10 * elements * HEAD_DIM,
            bytes_accessed=6 * tokens * width + 8 * tokens * kv_width,
            transcendentals=elements,
        ),
    )(queries, key_heads, value_heads, out_grad, ids_rows)


def solution(mesh):
    rows = P(("dp", "sp"), None)
    return jax.shard_map(
        body,
        mesh=mesh,
        in_specs=(rows, rows, rows, rows, P(("dp", "sp"))),
        out_specs=(rows, rows, rows),
        check_vma=False,
    )
```

```python
import functools

import jax
import jax.numpy as jnp
from jax import lax
from jax.experimental import pallas as pl
from jax.experimental.pallas import tpu as pltpu
from jax.sharding import PartitionSpec as P

HEAD_DIM = 128
MOST = 512
REACH = 4
SLOTS = REACH + 1
LOG2E = 1.4426950408889634
NT = (((1,), (1,)), ((), ()))


def kernel(
    n, kv_count, group,
    q_hbm, k_hbm, v_hbm, g_hbm, ids_ref,
    dq_ref, dk_ref, dv_ref,
    q_ref, g_ref, kv, ids, bias, scores, prods, probs, grads, part, out_buf, in_buf,
    fetch_sem,
    kv_send, kv_recv, back_send, back_recv, ids_send, ids_recv,
):
    me = lax.axis_index("sp")
    odd = lax.rem(me, 2) == 1
    tokens = q_hbm.shape[0]
    span = SLOTS * tokens
    scale = HEAD_DIM ** (-0.5)
    up = me + 2 < n
    partner = jnp.where(odd, me - 1, me + 1)

    def kv_copy(c, src, dst, which, target):
        return pltpu.make_async_remote_copy(
            src_ref=kv.at[c, src],
            dst_ref=kv.at[c, dst],
            send_sem=kv_send.at[c, which],
            recv_sem=kv_recv.at[c, dst - 1],
            device_id={"sp": target},
            device_id_type=pl.DeviceIdType.MESH,
        )

    def back_copy(c, slot, target):
        return pltpu.make_async_remote_copy(
            src_ref=out_buf.at[c, slot - 1],
            dst_ref=in_buf.at[c, slot - 1],
            send_sem=back_send.at[c, slot - 1],
            recv_sem=back_recv.at[c, slot - 1],
            device_id={"sp": target},
            device_id_type=pl.DeviceIdType.MESH,
        )

    def ids_copy(d):
        return pltpu.make_async_remote_copy(
            src_ref=ids_ref,
            dst_ref=ids.at[d],
            send_sem=ids_send.at[d - 1],
            recv_sem=ids_recv.at[d - 1],
            device_id={"sp": me + d},
            device_id_type=pl.DeviceIdType.MESH,
        )

    barrier = pltpu.get_barrier_semaphore()
    for d in range(1, SLOTS):
        @pl.when(me >= d)
        def _():
            pl.semaphore_signal(
                barrier, inc=1, device_id={"sp": me - d}, device_id_type=pl.DeviceIdType.MESH
            )

        @pl.when(me + d < n)
        def _():
            pl.semaphore_signal(
                barrier, inc=1, device_id={"sp": me + d}, device_id_type=pl.DeviceIdType.MESH
            )

    def fetch(c, what):
        if what < 2:
            cols = pl.ds(pl.multiple_of(c * HEAD_DIM, HEAD_DIM), HEAD_DIM)
            return pltpu.make_async_copy(
                (k_hbm, v_hbm)[what].at[:, cols], kv.at[c, 0, what], fetch_sem.at[c, what]
            )
        width = group * HEAD_DIM
        cols = pl.ds(pl.multiple_of(c * width, width), width)
        source, target = ((q_hbm, q_ref), (g_hbm, g_ref))[what - 2]
        return pltpu.make_async_copy(source.at[:, cols], target.at[c], fetch_sem.at[c, what])

    def start_fetch(c, first):
        fetch(c, first).start()
        fetch(c, first + 1).start()
        return 0

    lax.fori_loop(0, kv_count, lambda c, _: start_fetch(c, 0), 0)
    lax.fori_loop(0, kv_count, lambda c, _: start_fetch(c, 2), 0)

    def fill(c, _):
        for d in range(1, SLOTS):
            @pl.when(me < d)
            def _():
                kv[c, d] = jnp.zeros((2, tokens, HEAD_DIM), kv.dtype)
        return 0

    lax.fori_loop(0, kv_count, fill, 0)
    ids[0] = ids_ref[...]
    for d in range(1, SLOTS):
        @pl.when(me < d)
        def _():
            ids[d] = jnp.full(ids_ref.shape, -1, jnp.int32)

    pl.semaphore_wait(barrier, jnp.minimum(me, REACH) + jnp.minimum(n - 1 - me, REACH))

    def send_own(c):
        fetch(c, 0).wait()
        fetch(c, 1).wait()

        @pl.when(up)
        def _():
            kv_copy(c, 0, 2, 0, me + 2).start()

        @pl.when(jnp.logical_not(odd))
        def _():
            kv_copy(c, 0, 1, 2, me + 1).start()

    for d in range(1, SLOTS):
        @pl.when(me + d < n)
        def _():
            ids_copy(d).start()

    ahead = min(2, kv_count)
    for c in range(ahead):
        send_own(c)

    for d in range(1, SLOTS):
        @pl.when(me >= d)
        def _():
            ids_copy(d).wait_recv()

    row = jnp.broadcast_to(ids[0, 0:1, :].astype(jnp.float32), (tokens, tokens))
    for d in range(SLOTS):
        col = jnp.broadcast_to(ids[d, 0:1, :].astype(jnp.float32), (tokens, tokens)).T
        same = col == row
        if d == 0:
            key_at = lax.broadcasted_iota(jnp.int32, (tokens, tokens), 0)
            query_at = lax.broadcasted_iota(jnp.int32, (tokens, tokens), 1)
            same = same & (key_at <= query_at)
        bias[d * tokens:(d + 1) * tokens, :] = jnp.where(same, 0.0, -1e30)

    def stack(ref, c, first, count):
        cols = [ref[c, :, (first + i) * HEAD_DIM:(first + i + 1) * HEAD_DIM] for i in range(count)]
        return jnp.concatenate(cols, axis=0)

    def fold(array, combine):
        rows = [array[8 * i:8 * (i + 1)] for i in range(array.shape[0] // 8)]
        while len(rows) > 1:
            rows = [combine(rows[i], rows[i + 1]) for i in range(0, len(rows), 2)]
        return rows[0]

    factor = scale * LOG2E
    tile = 64

    def compute(c):
        fetch(c, 2).wait()
        fetch(c, 3).wait()
        keys = kv[c, :, 0].reshape(span, HEAD_DIM)
        values = kv[c, :, 1].reshape(span, HEAD_DIM)
        for pair in range(group // 2):
            lanes = slice(pair * 2 * tokens, (pair + 1) * 2 * tokens)
            q_pair = stack(q_ref, c, 2 * pair, 2)
            g_pair = stack(g_ref, c, 2 * pair, 2)
            s_all = lax.dot_general(keys, q_pair, NT, preferred_element_type=jnp.float32)
            tops = []
            for at in range(0, span, tile):
                blocked = bias[at:at + tile, :]
                s = s_all[at:at + tile] + jnp.concatenate([blocked, blocked], axis=1)
                scores[at:at + tile, lanes] = s
                tops.append(fold(s, jnp.maximum))
            top = jnp.max(functools.reduce(jnp.maximum, tops), axis=0, keepdims=True) * factor
            dp_all = lax.dot_general(values, g_pair, NT, preferred_element_type=jnp.float32)
            sums, dots = [], []
            for at in range(0, span, tile):
                e = jnp.exp2(scores[at:at + tile, lanes] * factor - top)
                dp = dp_all[at:at + tile]
                scores[at:at + tile, lanes] = e
                prods[at:at + tile, lanes] = dp
                sums.append(fold(e, jnp.add))
                dots.append(fold(e * dp, jnp.add))
            total = jnp.sum(functools.reduce(jnp.add, sums), axis=0, keepdims=True)
            inverse = 1.0 / total
            delta = jnp.sum(functools.reduce(jnp.add, dots), axis=0, keepdims=True) * inverse
            for at in range(0, span, tile):
                p = scores[at:at + tile, lanes] * inverse
                probs[at:at + tile, lanes] = p.astype(jnp.bfloat16)
                ds = p * (prods[at:at + tile, lanes] - delta)
                grads[at:at + tile, lanes] = ds.astype(jnp.bfloat16)
        dv = jnp.dot(probs[...], stack(g_ref, c, 0, group), preferred_element_type=jnp.float32)
        dk = scale * jnp.dot(
            grads[...], stack(q_ref, c, 0, group), preferred_element_type=jnp.float32
        )
        for d in range(SLOTS):
            for which, array in ((0, dk), (1, dv)):
                block = array[d * tokens:(d + 1) * tokens]
                if d <= 2:
                    part[c, d, which] = block
                else:
                    out_buf[c, d - 1, which] = block.astype(jnp.bfloat16)
        @pl.when(me >= 3)
        def _():
            back_copy(c, 3, me - 2).start()

        @pl.when(me >= 4)
        def _():
            back_copy(c, 4, me - 2).start()

        dq_t = scale * jnp.dot(keys.T, grads[...], preferred_element_type=jnp.float32)
        for h in range(group):
            cols = pl.ds(pl.multiple_of((c * group + h) * HEAD_DIM, HEAD_DIM), HEAD_DIM)
            dq_ref[:, cols] = dq_t[:, h * tokens:(h + 1) * tokens].T.astype(jnp.bfloat16)

    def step(t, _):
        @pl.when(t < kv_count)
        def _():
            @pl.when(t + ahead < kv_count)
            def _():
                send_own(t + ahead)

            @pl.when(me >= 2)
            def _():
                kv_copy(t, 0, 2, 0, me).wait_recv()

                @pl.when(up)
                def _():
                    kv_copy(t, 2, 4, 1, me + 2).start()

                @pl.when(odd)
                def _():
                    kv_copy(t, 2, 1, 2, me - 1).start()

        @pl.when((t >= 1) & (t - 1 < kv_count))
        def _():
            @pl.when(me >= 1)
            def _():
                kv_copy(t - 1, 0, 1, 2, me).wait_recv()

                @pl.when(up)
                def _():
                    kv_copy(t - 1, 1, 3, 3, me + 2).start()

        @pl.when((t >= 2) & (t - 2 < kv_count))
        def _():
            @pl.when(me >= 3)
            def _():
                kv_copy(t - 2, 1, 3, 3, me).wait_recv()

            @pl.when(me >= 4)
            def _():
                kv_copy(t - 2, 2, 4, 1, me).wait_recv()

            compute(t - 2)

        @pl.when((t >= 3) & (t - 3 < kv_count))
        def _():
            c = t - 3

            @pl.when(up & (me >= 1))
            def _():
                back_copy(c, 3, me).wait_recv()
                part[c, 1] += in_buf[c, 2].astype(jnp.float32)

            @pl.when(up & (me >= 2))
            def _():
                back_copy(c, 4, me).wait_recv()
                part[c, 2] += in_buf[c, 3].astype(jnp.float32)

            @pl.when(me >= 1)
            def _():
                out_buf[c, 0] = part[c, 1].astype(jnp.bfloat16)
                back_copy(c, 1, partner).start()

        @pl.when((t >= 4) & (t - 4 < kv_count))
        def _():
            c = t - 4

            @pl.when(odd & (me >= 3))
            def _():
                back_copy(c, 1, me).wait_recv()
                part[c, 2] += in_buf[c, 0].astype(jnp.float32)

            @pl.when(jnp.logical_not(odd))
            def _():
                back_copy(c, 1, me).wait_recv()
                part[c, 0] += in_buf[c, 0].astype(jnp.float32)

            @pl.when(me >= 2)
            def _():
                out_buf[c, 1] = part[c, 2].astype(jnp.bfloat16)
                back_copy(c, 2, me - 2).start()

        @pl.when(t >= 5)
        def _():
            c = t - 5

            @pl.when(up)
            def _():
                back_copy(c, 2, me).wait_recv()
                part[c, 0] += in_buf[c, 1].astype(jnp.float32)

            cols = pl.ds(pl.multiple_of(c * HEAD_DIM, HEAD_DIM), HEAD_DIM)
            dk_ref[:, cols] = part[c, 0, 0].astype(jnp.bfloat16)
            dv_ref[:, cols] = part[c, 0, 1].astype(jnp.bfloat16)

        return 0

    lax.fori_loop(0, kv_count + 5, step, 0)

    def drain(c, _):
        @pl.when(up)
        def _():
            kv_copy(c, 0, 2, 0, me).wait_send()

            @pl.when(me >= 2)
            def _():
                kv_copy(c, 2, 4, 1, me).wait_send()

            @pl.when(me >= 1)
            def _():
                kv_copy(c, 1, 3, 3, me).wait_send()

        @pl.when(jnp.logical_not(odd) | (me >= 3))
        def _():
            kv_copy(c, 0, 1, 2, me).wait_send()

        for slot in range(1, SLOTS):
            @pl.when(me >= slot)
            def _():
                back_copy(c, slot, me).wait_send()
        return 0

    lax.fori_loop(0, kv_count, drain, 0)
    for d in range(1, SLOTS):
        @pl.when(me + d < n)
        def _():
            ids_copy(d).wait_send()


def body(queries, key_heads, value_heads, out_grad, segment_ids):
    tokens, width = queries.shape
    kv_width = key_heads.shape[1]
    kv_count = kv_width // HEAD_DIM
    group = width // kv_width
    n = lax.axis_size("sp")
    assert -(-(MOST - 1) // tokens) == REACH and n % 2 == 0 and group % 2 == 0
    ids_rows = jnp.broadcast_to(segment_ids[None, :], (8, tokens))
    span = SLOTS * tokens
    vmem = pl.BlockSpec(memory_space=pltpu.VMEM)
    pairs = (kv_count, REACH, 2, tokens, HEAD_DIM)
    dma = pltpu.SemaphoreType.DMA
    elements = kv_count * group * tokens * span
    return pl.pallas_call(
        functools.partial(kernel, n, kv_count, group),
        out_shape=(
            jax.ShapeDtypeStruct((tokens, width), jnp.bfloat16),
            jax.ShapeDtypeStruct((tokens, kv_width), jnp.bfloat16),
            jax.ShapeDtypeStruct((tokens, kv_width), jnp.bfloat16),
        ),
        in_specs=[pl.BlockSpec(memory_space=pltpu.HBM)] * 4 + [vmem],
        out_specs=(vmem, vmem, vmem),
        scratch_shapes=[
            pltpu.VMEM((kv_count, tokens, group * HEAD_DIM), jnp.bfloat16),
            pltpu.VMEM((kv_count, tokens, group * HEAD_DIM), jnp.bfloat16),
            pltpu.VMEM((kv_count, SLOTS, 2, tokens, HEAD_DIM), jnp.bfloat16),
            pltpu.VMEM((SLOTS, 8, tokens), jnp.int32),
            pltpu.VMEM((span, tokens), jnp.float32),
            pltpu.VMEM((span, group * tokens), jnp.float32),
            pltpu.VMEM((span, group * tokens), jnp.float32),
            pltpu.VMEM((span, group * tokens), jnp.bfloat16),
            pltpu.VMEM((span, group * tokens), jnp.bfloat16),
            pltpu.VMEM((kv_count, 3, 2, tokens, HEAD_DIM), jnp.float32),
            pltpu.VMEM(pairs, jnp.bfloat16),
            pltpu.VMEM(pairs, jnp.bfloat16),
            dma((kv_count, 4)),
            dma((kv_count, 4)),
            dma((kv_count, REACH)),
            dma((kv_count, REACH)),
            dma((kv_count, REACH)),
            dma((REACH,)),
            dma((REACH,)),
        ],
        compiler_params=pltpu.CompilerParams(
            collective_id=0, has_side_effects=True, vmem_limit_bytes=48 * 1024 * 1024
        ),
        cost_estimate=pl.CostEstimate(
            flops=10 * elements * HEAD_DIM,
            bytes_accessed=6 * tokens * width + 8 * tokens * kv_width,
            transcendentals=elements,
        ),
    )(queries, key_heads, value_heads, out_grad, ids_rows)


def solution(mesh):
    rows = P(("dp", "sp"), None)
    return jax.shard_map(
        body,
        mesh=mesh,
        in_specs=(rows, rows, rows, rows, P(("dp", "sp"))),
        out_specs=(rows, rows, rows),
        check_vma=False,
    )
```

```python
import functools

import jax
import jax.numpy as jnp
from jax import lax
from jax.experimental import pallas as pl
from jax.experimental.pallas import tpu as pltpu
from jax.sharding import PartitionSpec as P

HEAD_DIM = 128
MOST = 512
REACH = 4
SLOTS = REACH + 1
LOG2E = 1.4426950408889634
NT = (((1,), (1,)), ((), ()))


def kernel(
    n, kv_count, group,
    q_hbm, k_hbm, v_hbm, g_hbm, ids_ref,
    dq_ref, dk_ref, dv_ref,
    q_ref, g_ref, kv, ids, own, bias, scores, prods, probs, grads, part, out_buf, in_buf,
    fetch_sem,
    kv_send, kv_recv, back_send, back_recv, ids_send, ids_recv,
):
    me = lax.axis_index("sp")
    odd = lax.rem(me, 2) == 1
    tokens = q_hbm.shape[0]
    span = SLOTS * tokens
    scale = HEAD_DIM ** (-0.5)
    up = me + 2 < n
    partner = jnp.where(odd, me - 1, me + 1)

    def kv_copy(c, src, dst, which, target):
        return pltpu.make_async_remote_copy(
            src_ref=kv.at[c, src],
            dst_ref=kv.at[c, dst],
            send_sem=kv_send.at[c, which],
            recv_sem=kv_recv.at[c, dst - 1],
            device_id={"sp": target},
            device_id_type=pl.DeviceIdType.MESH,
        )

    def back_copy(c, slot, target):
        return pltpu.make_async_remote_copy(
            src_ref=out_buf.at[c, slot - 1],
            dst_ref=in_buf.at[c, slot - 1],
            send_sem=back_send.at[c, slot - 1],
            recv_sem=back_recv.at[c, slot - 1],
            device_id={"sp": target},
            device_id_type=pl.DeviceIdType.MESH,
        )

    def ids_copy(d):
        return pltpu.make_async_remote_copy(
            src_ref=ids_ref,
            dst_ref=ids.at[d],
            send_sem=ids_send.at[d - 1],
            recv_sem=ids_recv.at[d - 1],
            device_id={"sp": me + d},
            device_id_type=pl.DeviceIdType.MESH,
        )

    barrier = pltpu.get_barrier_semaphore()
    for d in range(1, SLOTS):
        @pl.when(me >= d)
        def _():
            pl.semaphore_signal(
                barrier, inc=1, device_id={"sp": me - d}, device_id_type=pl.DeviceIdType.MESH
            )

        @pl.when(me + d < n)
        def _():
            pl.semaphore_signal(
                barrier, inc=1, device_id={"sp": me + d}, device_id_type=pl.DeviceIdType.MESH
            )

    def fetch(c, what):
        if what < 2:
            cols = pl.ds(pl.multiple_of(c * HEAD_DIM, HEAD_DIM), HEAD_DIM)
            return pltpu.make_async_copy(
                (k_hbm, v_hbm)[what].at[:, cols], kv.at[c, 0, what], fetch_sem.at[c, what]
            )
        width = group * HEAD_DIM
        cols = pl.ds(pl.multiple_of(c * width, width), width)
        source, target = ((q_hbm, q_ref), (g_hbm, g_ref))[what - 2]
        return pltpu.make_async_copy(source.at[:, cols], target.at[c], fetch_sem.at[c, what])

    def start_fetch(c, first):
        fetch(c, first).start()
        fetch(c, first + 1).start()
        return 0

    lax.fori_loop(0, kv_count, lambda c, _: start_fetch(c, 0), 0)
    lax.fori_loop(0, kv_count, lambda c, _: start_fetch(c, 2), 0)

    def fill(c, _):
        for d in range(1, SLOTS):
            @pl.when(me < d)
            def _():
                kv[c, d] = jnp.zeros((2, tokens, HEAD_DIM), kv.dtype)
        return 0

    lax.fori_loop(0, kv_count, fill, 0)
    ids[0] = ids_ref[...]
    for d in range(1, SLOTS):
        @pl.when(me < d)
        def _():
            ids[d] = jnp.full(ids_ref.shape, -1, jnp.int32)

    pl.semaphore_wait(barrier, jnp.minimum(me, REACH) + jnp.minimum(n - 1 - me, REACH))

    def send_own(c):
        fetch(c, 0).wait()
        fetch(c, 1).wait()

        @pl.when(up)
        def _():
            kv_copy(c, 0, 2, 0, me + 2).start()

        @pl.when(jnp.logical_not(odd))
        def _():
            kv_copy(c, 0, 1, 2, me + 1).start()

    for d in range(1, SLOTS):
        @pl.when(me + d < n)
        def _():
            ids_copy(d).start()

    ahead = min(2, kv_count)
    for c in range(ahead):
        send_own(c)

    for d in range(1, SLOTS):
        @pl.when(me >= d)
        def _():
            ids_copy(d).wait_recv()

    key_at = lax.broadcasted_iota(jnp.int32, (tokens, tokens), 0)
    query_at = lax.broadcasted_iota(jnp.int32, (tokens, tokens), 1)
    row = jnp.broadcast_to(ids[0, 0:1, :].astype(jnp.float32), (tokens, tokens))
    own[...] = (key_at <= query_at).astype(jnp.float32)

    def ids_of(d):
        return jnp.broadcast_to(ids[d, 0:1, :].astype(jnp.float32), (tokens, tokens)).T

    for d in range(REACH):
        col = jnp.where(own[...] > 0.0, ids_of(0), ids_of(REACH)) if d == 0 else ids_of(d)
        bias[d * tokens:(d + 1) * tokens, :] = jnp.where(col == row, 0.0, -1e30)

    def stack(ref, c, first, count):
        cols = [ref[c, :, (first + i) * HEAD_DIM:(first + i + 1) * HEAD_DIM] for i in range(count)]
        return jnp.concatenate(cols, axis=0)

    def fold(array, combine):
        rows = [array[8 * i:8 * (i + 1)] for i in range(array.shape[0] // 8)]
        while len(rows) > 1:
            rows = [combine(rows[i], rows[i + 1]) for i in range(0, len(rows), 2)]
        return rows[0]

    factor = scale * LOG2E
    tile = 64
    last = REACH * tokens

    def twice(array):
        return jnp.concatenate([array, array], axis=1)

    def merged(array, at):
        block = array[at:at + tile]
        if at < tokens:
            block = jnp.where(
                twice(own[at:at + tile, :]) > 0.0, block, array[last + at:last + at + tile]
            )
        return block

    def put(ref, at, lanes, block):
        if at < tokens:
            mine = twice(own[at:at + tile, :]) > 0.0
            ref[at:at + tile, lanes] = jnp.where(mine, block, 0.0).astype(jnp.bfloat16)
            ref[last + at:last + at + tile, lanes] = jnp.where(mine, 0.0, block).astype(
                jnp.bfloat16
            )
        else:
            ref[at:at + tile, lanes] = block.astype(jnp.bfloat16)

    def lanes_of(pair):
        return slice(pair * 2 * tokens, (pair + 1) * 2 * tokens)

    def score_pass(c, pair):
        keys = kv[c, :, 0].reshape(span, HEAD_DIM)
        q_pair = stack(q_ref, c, 2 * pair, 2)
        s_all = lax.dot_general(keys, q_pair, NT, preferred_element_type=jnp.float32)
        tops = []
        for at in range(0, last, tile):
            s = merged(s_all, at) + twice(bias[at:at + tile, :])
            scores[at:at + tile, lanes_of(pair)] = s
            tops.append(fold(s, jnp.maximum))
        return jnp.max(functools.reduce(jnp.maximum, tops), axis=0, keepdims=True) * factor

    def exp_pass(c, pair, top):
        lanes = lanes_of(pair)
        values = kv[c, :, 1].reshape(span, HEAD_DIM)
        g_pair = stack(g_ref, c, 2 * pair, 2)
        dp_all = lax.dot_general(values, g_pair, NT, preferred_element_type=jnp.float32)
        sums, dots = [], []
        for at in range(0, last, tile):
            e = jnp.exp2(scores[at:at + tile, lanes] * factor - top)
            dp = merged(dp_all, at)
            scores[at:at + tile, lanes] = e
            prods[at:at + tile, lanes] = dp
            sums.append(fold(e, jnp.add))
            dots.append(fold(e * dp, jnp.add))
        inverse = 1.0 / jnp.sum(functools.reduce(jnp.add, sums), axis=0, keepdims=True)
        delta = jnp.sum(functools.reduce(jnp.add, dots), axis=0, keepdims=True) * inverse
        return inverse, delta

    def grad_pass(pair, inverse, delta):
        lanes = lanes_of(pair)
        for at in range(0, last, tile):
            p = scores[at:at + tile, lanes] * inverse
            put(probs, at, lanes, p)
            put(grads, at, lanes, p * (prods[at:at + tile, lanes] - delta))

    def compute(c):
        fetch(c, 2).wait()
        fetch(c, 3).wait()
        pairs = group // 2
        tops, rest = {}, {}
        for at in range(pairs + 2):
            if at < pairs:
                tops[at] = score_pass(c, at)
            if 1 <= at <= pairs:
                rest[at - 1] = exp_pass(c, at - 1, tops[at - 1])
            if at >= 2:
                grad_pass(at - 2, *rest[at - 2])
        keys = kv[c, :, 0].reshape(span, HEAD_DIM)
        dv = jnp.dot(probs[...], stack(g_ref, c, 0, group), preferred_element_type=jnp.float32)
        dk = scale * jnp.dot(
            grads[...], stack(q_ref, c, 0, group), preferred_element_type=jnp.float32
        )
        for d in range(SLOTS):
            for which, array in ((0, dk), (1, dv)):
                block = array[d * tokens:(d + 1) * tokens]
                if d <= 2:
                    part[c, d, which] = block
                else:
                    out_buf[c, d - 1, which] = block.astype(jnp.bfloat16)
        @pl.when(me >= 3)
        def _():
            back_copy(c, 3, me - 2).start()

        @pl.when(me >= 4)
        def _():
            back_copy(c, 4, me - 2).start()

        dq_t = scale * jnp.dot(keys.T, grads[...], preferred_element_type=jnp.float32)
        for h in range(group):
            cols = pl.ds(pl.multiple_of((c * group + h) * HEAD_DIM, HEAD_DIM), HEAD_DIM)
            dq_ref[:, cols] = dq_t[:, h * tokens:(h + 1) * tokens].T.astype(jnp.bfloat16)

    def step(t, _):
        @pl.when(t < kv_count)
        def _():
            @pl.when(t + ahead < kv_count)
            def _():
                send_own(t + ahead)

            @pl.when(me >= 2)
            def _():
                kv_copy(t, 0, 2, 0, me).wait_recv()

                @pl.when(up)
                def _():
                    kv_copy(t, 2, 4, 1, me + 2).start()

                @pl.when(odd)
                def _():
                    kv_copy(t, 2, 1, 2, me - 1).start()

        @pl.when((t >= 1) & (t - 1 < kv_count))
        def _():
            @pl.when(me >= 1)
            def _():
                kv_copy(t - 1, 0, 1, 2, me).wait_recv()

                @pl.when(up)
                def _():
                    kv_copy(t - 1, 1, 3, 3, me + 2).start()

        @pl.when((t >= 2) & (t - 2 < kv_count))
        def _():
            @pl.when(me >= 3)
            def _():
                kv_copy(t - 2, 1, 3, 3, me).wait_recv()

            @pl.when(me >= 4)
            def _():
                kv_copy(t - 2, 2, 4, 1, me).wait_recv()

            compute(t - 2)

        @pl.when((t >= 3) & (t - 3 < kv_count))
        def _():
            c = t - 3

            @pl.when(up & (me >= 1))
            def _():
                back_copy(c, 3, me).wait_recv()
                part[c, 1] += in_buf[c, 2].astype(jnp.float32)

            @pl.when(up & (me >= 2))
            def _():
                back_copy(c, 4, me).wait_recv()
                part[c, 2] += in_buf[c, 3].astype(jnp.float32)

            @pl.when(me >= 1)
            def _():
                out_buf[c, 0] = part[c, 1].astype(jnp.bfloat16)
                back_copy(c, 1, partner).start()

        @pl.when((t >= 4) & (t - 4 < kv_count))
        def _():
            c = t - 4

            @pl.when(odd & (me >= 3))
            def _():
                back_copy(c, 1, me).wait_recv()
                part[c, 2] += in_buf[c, 0].astype(jnp.float32)

            @pl.when(jnp.logical_not(odd))
            def _():
                back_copy(c, 1, me).wait_recv()
                part[c, 0] += in_buf[c, 0].astype(jnp.float32)

            @pl.when(me >= 2)
            def _():
                out_buf[c, 1] = part[c, 2].astype(jnp.bfloat16)
                back_copy(c, 2, me - 2).start()

        @pl.when(t >= 5)
        def _():
            c = t - 5

            @pl.when(up)
            def _():
                back_copy(c, 2, me).wait_recv()
                part[c, 0] += in_buf[c, 1].astype(jnp.float32)

            cols = pl.ds(pl.multiple_of(c * HEAD_DIM, HEAD_DIM), HEAD_DIM)
            dk_ref[:, cols] = part[c, 0, 0].astype(jnp.bfloat16)
            dv_ref[:, cols] = part[c, 0, 1].astype(jnp.bfloat16)

        return 0

    lax.fori_loop(0, kv_count + 5, step, 0)

    def drain(c, _):
        @pl.when(up)
        def _():
            kv_copy(c, 0, 2, 0, me).wait_send()

            @pl.when(me >= 2)
            def _():
                kv_copy(c, 2, 4, 1, me).wait_send()

            @pl.when(me >= 1)
            def _():
                kv_copy(c, 1, 3, 3, me).wait_send()

        @pl.when(jnp.logical_not(odd) | (me >= 3))
        def _():
            kv_copy(c, 0, 1, 2, me).wait_send()

        for slot in range(1, SLOTS):
            @pl.when(me >= slot)
            def _():
                back_copy(c, slot, me).wait_send()
        return 0

    lax.fori_loop(0, kv_count, drain, 0)
    for d in range(1, SLOTS):
        @pl.when(me + d < n)
        def _():
            ids_copy(d).wait_send()


def body(queries, key_heads, value_heads, out_grad, segment_ids):
    tokens, width = queries.shape
    kv_width = key_heads.shape[1]
    kv_count = kv_width // HEAD_DIM
    group = width // kv_width
    n = lax.axis_size("sp")
    assert -(-(MOST - 1) // tokens) == REACH and n % 2 == 0 and group % 2 == 0
    ids_rows = jnp.broadcast_to(segment_ids[None, :], (8, tokens))
    span = SLOTS * tokens
    vmem = pl.BlockSpec(memory_space=pltpu.VMEM)
    pairs = (kv_count, REACH, 2, tokens, HEAD_DIM)
    dma = pltpu.SemaphoreType.DMA
    elements = kv_count * group * tokens * span
    return pl.pallas_call(
        functools.partial(kernel, n, kv_count, group),
        out_shape=(
            jax.ShapeDtypeStruct((tokens, width), jnp.bfloat16),
            jax.ShapeDtypeStruct((tokens, kv_width), jnp.bfloat16),
            jax.ShapeDtypeStruct((tokens, kv_width), jnp.bfloat16),
        ),
        in_specs=[pl.BlockSpec(memory_space=pltpu.HBM)] * 4 + [vmem],
        out_specs=(vmem, vmem, vmem),
        scratch_shapes=[
            pltpu.VMEM((kv_count, tokens, group * HEAD_DIM), jnp.bfloat16),
            pltpu.VMEM((kv_count, tokens, group * HEAD_DIM), jnp.bfloat16),
            pltpu.VMEM((kv_count, SLOTS, 2, tokens, HEAD_DIM), jnp.bfloat16),
            pltpu.VMEM((SLOTS, 8, tokens), jnp.int32),
            pltpu.VMEM((tokens, tokens), jnp.float32),
            pltpu.VMEM((REACH * tokens, tokens), jnp.float32),
            pltpu.VMEM((REACH * tokens, group * tokens), jnp.float32),
            pltpu.VMEM((REACH * tokens, group * tokens), jnp.float32),
            pltpu.VMEM((span, group * tokens), jnp.bfloat16),
            pltpu.VMEM((span, group * tokens), jnp.bfloat16),
            pltpu.VMEM((kv_count, 3, 2, tokens, HEAD_DIM), jnp.float32),
            pltpu.VMEM(pairs, jnp.bfloat16),
            pltpu.VMEM(pairs, jnp.bfloat16),
            dma((kv_count, 4)),
            dma((kv_count, 4)),
            dma((kv_count, REACH)),
            dma((kv_count, REACH)),
            dma((kv_count, REACH)),
            dma((REACH,)),
            dma((REACH,)),
        ],
        compiler_params=pltpu.CompilerParams(
            collective_id=0, has_side_effects=True, vmem_limit_bytes=61 * 1024 * 1024
        ),
        cost_estimate=pl.CostEstimate(
            flops=10 * elements * HEAD_DIM,
            bytes_accessed=6 * tokens * width + 8 * tokens * kv_width,
            transcendentals=elements,
        ),
    )(queries, key_heads, value_heads, out_grad, ids_rows)


def solution(mesh):
    rows = P(("dp", "sp"), None)
    return jax.shard_map(
        body,
        mesh=mesh,
        in_specs=(rows, rows, rows, rows, P(("dp", "sp"))),
        out_specs=(rows, rows, rows),
        check_vma=False,
    )
```

```python
import functools

import jax
import jax.numpy as jnp
from jax import lax
from jax.experimental import pallas as pl
from jax.experimental.pallas import tpu as pltpu
from jax.sharding import PartitionSpec as P

HEAD_DIM = 128
MOST = 512
REACH = 4
SLOTS = REACH + 1
LOG2E = 1.4426950408889634
NT = (((1,), (1,)), ((), ()))


def kernel(
    n, kv_count, group,
    q_hbm, k_hbm, v_hbm, g_hbm, ids_ref,
    dq_hbm, dk_hbm, dv_hbm,
    q_ref, g_ref, kv, ids, own, bias, scores, prods, probs, grads, part, out_buf, in_buf,
    dq_ref, dkv_ref, fetch_sem, store_sem,
    kv_send, kv_recv, back_send, back_recv, ids_send, ids_recv,
):
    me = lax.axis_index("sp")
    odd = lax.rem(me, 2) == 1
    tokens = q_hbm.shape[0]
    span = SLOTS * tokens
    scale = HEAD_DIM ** (-0.5)
    up = me + 2 < n
    partner = jnp.where(odd, me - 1, me + 1)

    def kv_copy(c, src, dst, which, target):
        return pltpu.make_async_remote_copy(
            src_ref=kv.at[c, src],
            dst_ref=kv.at[c, dst],
            send_sem=kv_send.at[c, which],
            recv_sem=kv_recv.at[c, dst - 1],
            device_id={"sp": target},
            device_id_type=pl.DeviceIdType.MESH,
        )

    def back_copy(c, slot, target):
        return pltpu.make_async_remote_copy(
            src_ref=out_buf.at[c, slot - 1],
            dst_ref=in_buf.at[c, slot - 1],
            send_sem=back_send.at[c, slot - 1],
            recv_sem=back_recv.at[c, slot - 1],
            device_id={"sp": target},
            device_id_type=pl.DeviceIdType.MESH,
        )

    def ids_copy(d):
        return pltpu.make_async_remote_copy(
            src_ref=ids_ref,
            dst_ref=ids.at[d],
            send_sem=ids_send.at[d - 1],
            recv_sem=ids_recv.at[d - 1],
            device_id={"sp": me + d},
            device_id_type=pl.DeviceIdType.MESH,
        )

    barrier = pltpu.get_barrier_semaphore()
    for d in range(1, SLOTS):
        @pl.when(me >= d)
        def _():
            pl.semaphore_signal(
                barrier, inc=1, device_id={"sp": me - d}, device_id_type=pl.DeviceIdType.MESH
            )

        @pl.when(me + d < n)
        def _():
            pl.semaphore_signal(
                barrier, inc=1, device_id={"sp": me + d}, device_id_type=pl.DeviceIdType.MESH
            )

    def fetch(c, what):
        if what < 2:
            cols = pl.ds(pl.multiple_of(c * HEAD_DIM, HEAD_DIM), HEAD_DIM)
            return pltpu.make_async_copy(
                (k_hbm, v_hbm)[what].at[:, cols], kv.at[c, 0, what], fetch_sem.at[c, what]
            )
        width = group * HEAD_DIM
        cols = pl.ds(pl.multiple_of(c * width, width), width)
        source, target = ((q_hbm, q_ref), (g_hbm, g_ref))[what - 2]
        return pltpu.make_async_copy(source.at[:, cols], target.at[c], fetch_sem.at[c, what])

    def store(c, what):
        if what < 2:
            cols = pl.ds(pl.multiple_of(c * HEAD_DIM, HEAD_DIM), HEAD_DIM)
            source, target = dkv_ref.at[c, what], (dk_hbm, dv_hbm)[what].at[:, cols]
        else:
            width = group * HEAD_DIM
            cols = pl.ds(pl.multiple_of(c * width, width), width)
            source, target = dq_ref.at[c], dq_hbm.at[:, cols]
        return pltpu.make_async_copy(source, target, store_sem.at[c, what])

    def start_fetch(c, first):
        fetch(c, first).start()
        fetch(c, first + 1).start()
        return 0

    lax.fori_loop(0, kv_count, lambda c, _: start_fetch(c, 0), 0)
    lax.fori_loop(0, kv_count, lambda c, _: start_fetch(c, 2), 0)

    def fill(c, _):
        for d in range(1, SLOTS):
            @pl.when(me < d)
            def _():
                kv[c, d] = jnp.zeros((2, tokens, HEAD_DIM), kv.dtype)
        return 0

    lax.fori_loop(0, kv_count, fill, 0)
    ids[0] = ids_ref[...]
    for d in range(1, SLOTS):
        @pl.when(me < d)
        def _():
            ids[d] = jnp.full(ids_ref.shape, -1, jnp.int32)

    pl.semaphore_wait(barrier, jnp.minimum(me, REACH) + jnp.minimum(n - 1 - me, REACH))

    def send_own(c):
        fetch(c, 0).wait()
        fetch(c, 1).wait()

        @pl.when(up)
        def _():
            kv_copy(c, 0, 2, 0, me + 2).start()

        @pl.when(jnp.logical_not(odd))
        def _():
            kv_copy(c, 0, 1, 2, me + 1).start()

    for d in range(1, SLOTS):
        @pl.when(me + d < n)
        def _():
            ids_copy(d).start()

    ahead = min(2, kv_count)
    for c in range(ahead):
        send_own(c)

    for d in range(1, SLOTS):
        @pl.when(me >= d)
        def _():
            ids_copy(d).wait_recv()

    key_at = lax.broadcasted_iota(jnp.int32, (tokens, tokens), 0)
    query_at = lax.broadcasted_iota(jnp.int32, (tokens, tokens), 1)
    row = jnp.broadcast_to(ids[0, 0:1, :].astype(jnp.float32), (tokens, tokens))
    own[...] = (key_at <= query_at).astype(jnp.float32)

    def ids_of(d):
        return jnp.broadcast_to(ids[d, 0:1, :].astype(jnp.float32), (tokens, tokens)).T

    for d in range(REACH):
        col = jnp.where(own[...] > 0.0, ids_of(0), ids_of(REACH)) if d == 0 else ids_of(d)
        bias[d * tokens:(d + 1) * tokens, :] = jnp.where(col == row, 0.0, -1e30)

    def stack(ref, c, first, count):
        cols = [ref[c, :, (first + i) * HEAD_DIM:(first + i + 1) * HEAD_DIM] for i in range(count)]
        return jnp.concatenate(cols, axis=0)

    def fold(array, combine):
        rows = [array[8 * i:8 * (i + 1)] for i in range(array.shape[0] // 8)]
        while len(rows) > 1:
            rows = [combine(rows[i], rows[i + 1]) for i in range(0, len(rows), 2)]
        return rows[0]

    factor = scale * LOG2E
    tile = 64
    last = REACH * tokens

    def twice(array):
        return jnp.concatenate([array, array], axis=1)

    def merged(array, at):
        block = array[at:at + tile]
        if at < tokens:
            block = jnp.where(
                twice(own[at:at + tile, :]) > 0.0, block, array[last + at:last + at + tile]
            )
        return block

    def put(ref, at, lanes, block):
        if at < tokens:
            mine = twice(own[at:at + tile, :]) > 0.0
            ref[at:at + tile, lanes] = jnp.where(mine, block, 0.0).astype(jnp.bfloat16)
            ref[last + at:last + at + tile, lanes] = jnp.where(mine, 0.0, block).astype(
                jnp.bfloat16
            )
        else:
            ref[at:at + tile, lanes] = block.astype(jnp.bfloat16)

    def lanes_of(pair):
        return slice(pair * 2 * tokens, (pair + 1) * 2 * tokens)

    def score_pass(c, pair):
        keys = kv[c, :, 0].reshape(span, HEAD_DIM)
        q_pair = stack(q_ref, c, 2 * pair, 2)
        s_all = lax.dot_general(keys, q_pair, NT, preferred_element_type=jnp.float32)
        tops = []
        for at in range(0, last, tile):
            s = merged(s_all, at) + twice(bias[at:at + tile, :])
            scores[at:at + tile, lanes_of(pair)] = s
            tops.append(fold(s, jnp.maximum))
        return jnp.max(functools.reduce(jnp.maximum, tops), axis=0, keepdims=True) * factor

    def exp_pass(c, pair, top):
        lanes = lanes_of(pair)
        values = kv[c, :, 1].reshape(span, HEAD_DIM)
        g_pair = stack(g_ref, c, 2 * pair, 2)
        dp_all = lax.dot_general(values, g_pair, NT, preferred_element_type=jnp.float32)
        sums, dots = [], []
        for at in range(0, last, tile):
            e = jnp.exp2(scores[at:at + tile, lanes] * factor - top)
            dp = merged(dp_all, at)
            scores[at:at + tile, lanes] = e
            prods[at:at + tile, lanes] = dp
            sums.append(fold(e, jnp.add))
            dots.append(fold(e * dp, jnp.add))
        inverse = 1.0 / jnp.sum(functools.reduce(jnp.add, sums), axis=0, keepdims=True)
        delta = jnp.sum(functools.reduce(jnp.add, dots), axis=0, keepdims=True) * inverse
        return inverse, delta

    def grad_pass(pair, inverse, delta):
        lanes = lanes_of(pair)
        for at in range(0, last, tile):
            p = scores[at:at + tile, lanes] * inverse
            put(probs, at, lanes, p)
            put(grads, at, lanes, p * (prods[at:at + tile, lanes] - delta))

    def first_half(c):
        fetch(c, 2).wait()
        fetch(c, 3).wait()
        pairs = group // 2
        tops, rest = {}, {}
        for at in range(pairs + 2):
            if at < pairs:
                tops[at] = score_pass(c, at)
            if 1 <= at <= pairs:
                rest[at - 1] = exp_pass(c, at - 1, tops[at - 1])
            if at >= 2:
                grad_pass(at - 2, *rest[at - 2])

    def second_half(c):
        dv = jnp.dot(probs[...], stack(g_ref, c, 0, group), preferred_element_type=jnp.float32)
        dk = scale * jnp.dot(
            grads[...], stack(q_ref, c, 0, group), preferred_element_type=jnp.float32
        )
        for d in range(SLOTS):
            for which, array in ((0, dk), (1, dv)):
                block = array[d * tokens:(d + 1) * tokens]
                if d <= 2:
                    part[c, d, which] = block
                else:
                    out_buf[c, d - 1, which] = block.astype(jnp.bfloat16)

        @pl.when(me >= 3)
        def _():
            back_copy(c, 3, me - 2).start()

        @pl.when(me >= 4)
        def _():
            back_copy(c, 4, me - 2).start()

        keys = kv[c, :, 0].reshape(span, HEAD_DIM)
        dq_t = scale * jnp.dot(keys.T, grads[...], preferred_element_type=jnp.float32)
        for h in range(group):
            dq_ref[c, :, h * HEAD_DIM:(h + 1) * HEAD_DIM] = (
                dq_t[:, h * tokens:(h + 1) * tokens].T.astype(jnp.bfloat16)
            )
        store(c, 2).start()

    def within(c):
        return (c >= 0) & (c < kv_count)

    def step(t, _):
        c = t - 2

        @pl.when(within(t - 1) & (me >= 1))
        def _():
            kv_copy(t - 1, 0, 1, 2, me).wait_recv()

            @pl.when(up)
            def _():
                kv_copy(t - 1, 1, 3, 3, me + 2).start()

        @pl.when(within(t) & (me >= 2))
        def _():
            kv_copy(t, 0, 2, 0, me).wait_recv()

            @pl.when(odd)
            def _():
                kv_copy(t, 2, 1, 2, me - 1).start()

            @pl.when(up)
            def _():
                kv_copy(t, 2, 4, 1, me + 2).start()

        @pl.when(within(c))
        def _():
            @pl.when(me >= 3)
            def _():
                kv_copy(c, 1, 3, 3, me).wait_recv()

            @pl.when(me >= 4)
            def _():
                kv_copy(c, 2, 4, 1, me).wait_recv()

            first_half(c)

        @pl.when(t + ahead < kv_count)
        def _():
            send_own(t + ahead)

        @pl.when(within(c - 2))
        def _():
            b = c - 2

            @pl.when(up & (me >= 1))
            def _():
                back_copy(b, 3, me).wait_recv()
                part[b, 1] += in_buf[b, 2].astype(jnp.float32)

            @pl.when(up & (me >= 2))
            def _():
                back_copy(b, 4, me).wait_recv()
                part[b, 2] += in_buf[b, 3].astype(jnp.float32)

            @pl.when(me >= 1)
            def _():
                out_buf[b, 0] = part[b, 1].astype(jnp.bfloat16)
                back_copy(b, 1, partner).start()

        @pl.when(within(c - 3))
        def _():
            b = c - 3

            @pl.when(odd & (me >= 3))
            def _():
                back_copy(b, 1, me).wait_recv()
                part[b, 2] += in_buf[b, 0].astype(jnp.float32)

            @pl.when(jnp.logical_not(odd))
            def _():
                back_copy(b, 1, me).wait_recv()
                part[b, 0] += in_buf[b, 0].astype(jnp.float32)

            @pl.when(me >= 2)
            def _():
                out_buf[b, 1] = part[b, 2].astype(jnp.bfloat16)
                back_copy(b, 2, me - 2).start()

        @pl.when(within(c - 5))
        def _():
            b = c - 5

            @pl.when(up)
            def _():
                back_copy(b, 2, me).wait_recv()
                part[b, 0] += in_buf[b, 1].astype(jnp.float32)

            dkv_ref[b] = part[b, 0].astype(jnp.bfloat16)
            store(b, 0).start()
            store(b, 1).start()

        @pl.when(within(c))
        def _():
            second_half(c)

        return 0

    lax.fori_loop(0, kv_count + 7, step, 0)

    def drain(c, _):
        @pl.when(up)
        def _():
            kv_copy(c, 0, 2, 0, me).wait_send()

            @pl.when(me >= 2)
            def _():
                kv_copy(c, 2, 4, 1, me).wait_send()

            @pl.when(me >= 1)
            def _():
                kv_copy(c, 1, 3, 3, me).wait_send()

        @pl.when(jnp.logical_not(odd) | (me >= 3))
        def _():
            kv_copy(c, 0, 1, 2, me).wait_send()

        for slot in range(1, SLOTS):
            @pl.when(me >= slot)
            def _():
                back_copy(c, slot, me).wait_send()
        for what in range(3):
            store(c, what).wait()
        return 0

    lax.fori_loop(0, kv_count, drain, 0)
    for d in range(1, SLOTS):
        @pl.when(me + d < n)
        def _():
            ids_copy(d).wait_send()


def finish(dq_in, dk_in, dv_in, dq_out, dk_out, dv_out, sems):
    tokens = dq_in.shape[0]
    part = tokens // 4
    copies = [
        pltpu.make_async_copy(
            dq_in.at[pl.ds(i * part, part)], dq_out.at[pl.ds(i * part, part)], sems.at[i]
        )
        for i in range(4)
    ]
    copies.append(pltpu.make_async_copy(dk_in, dk_out, sems.at[4]))
    copies.append(pltpu.make_async_copy(dv_in, dv_out, sems.at[5]))
    for copy in copies:
        copy.start()
    for copy in copies:
        copy.wait()


def body(queries, key_heads, value_heads, out_grad, segment_ids):
    tokens, width = queries.shape
    kv_width = key_heads.shape[1]
    kv_count = kv_width // HEAD_DIM
    group = width // kv_width
    n = lax.axis_size("sp")
    assert -(-(MOST - 1) // tokens) == REACH and n % 2 == 0 and group % 2 == 0
    ids_rows = jnp.broadcast_to(segment_ids[None, :], (8, tokens))
    span = SLOTS * tokens
    vmem = pl.BlockSpec(memory_space=pltpu.VMEM)
    pairs = (kv_count, REACH, 2, tokens, HEAD_DIM)
    dma = pltpu.SemaphoreType.DMA
    elements = kv_count * group * tokens * span
    shapes = (
        jax.ShapeDtypeStruct((tokens, width), jnp.bfloat16),
        jax.ShapeDtypeStruct((tokens, kv_width), jnp.bfloat16),
        jax.ShapeDtypeStruct((tokens, kv_width), jnp.bfloat16),
    )
    anywhere = pl.BlockSpec(memory_space=pl.ANY)
    grads = pl.pallas_call(
        functools.partial(kernel, n, kv_count, group),
        out_shape=shapes,
        in_specs=[pl.BlockSpec(memory_space=pltpu.HBM)] * 4 + [vmem],
        out_specs=(anywhere, anywhere, anywhere),
        scratch_shapes=[
            pltpu.VMEM((kv_count, tokens, group * HEAD_DIM), jnp.bfloat16),
            pltpu.VMEM((kv_count, tokens, group * HEAD_DIM), jnp.bfloat16),
            pltpu.VMEM((kv_count, SLOTS, 2, tokens, HEAD_DIM), jnp.bfloat16),
            pltpu.VMEM((SLOTS, 8, tokens), jnp.int32),
            pltpu.VMEM((tokens, tokens), jnp.float32),
            pltpu.VMEM((REACH * tokens, tokens), jnp.float32),
            pltpu.VMEM((REACH * tokens, group * tokens), jnp.float32),
            pltpu.VMEM((REACH * tokens, group * tokens), jnp.float32),
            pltpu.VMEM((span, group * tokens), jnp.bfloat16),
            pltpu.VMEM((span, group * tokens), jnp.bfloat16),
            pltpu.VMEM((kv_count, 3, 2, tokens, HEAD_DIM), jnp.float32),
            pltpu.VMEM(pairs, jnp.bfloat16),
            pltpu.VMEM(pairs, jnp.bfloat16),
            pltpu.VMEM((kv_count, tokens, group * HEAD_DIM), jnp.bfloat16),
            pltpu.VMEM((kv_count, 2, tokens, HEAD_DIM), jnp.bfloat16),
            dma((kv_count, 4)),
            dma((kv_count, 3)),
            dma((kv_count, 4)),
            dma((kv_count, REACH)),
            dma((kv_count, REACH)),
            dma((kv_count, REACH)),
            dma((REACH,)),
            dma((REACH,)),
        ],
        compiler_params=pltpu.CompilerParams(
            collective_id=0, has_side_effects=True, vmem_limit_bytes=61 * 1024 * 1024
        ),
        cost_estimate=pl.CostEstimate(
            flops=10 * elements * HEAD_DIM,
            bytes_accessed=6 * tokens * width + 8 * tokens * kv_width,
            transcendentals=elements,
        ),
    )(queries, key_heads, value_heads, out_grad, ids_rows)
    return pl.pallas_call(
        finish,
        out_shape=shapes,
        in_specs=[anywhere] * 3,
        out_specs=(anywhere, anywhere, anywhere),
        scratch_shapes=[dma((6,))],
        compiler_params=pltpu.CompilerParams(vmem_limit_bytes=61 * 1024 * 1024),
    )(*grads)


def solution(mesh):
    rows = P(("dp", "sp"), None)
    return jax.shard_map(
        body,
        mesh=mesh,
        in_specs=(rows, rows, rows, rows, P(("dp", "sp"))),
        out_specs=(rows, rows, rows),
        check_vma=False,
    )
```

```python
import functools

import jax
import jax.numpy as jnp
from jax import lax
from jax.experimental import pallas as pl
from jax.experimental.pallas import tpu as pltpu
from jax.sharding import PartitionSpec as P

HEAD_DIM = 128
MOST = 512
REACH = 4
SLOTS = REACH + 1
LOG2E = 1.4426950408889634
NT = (((1,), (1,)), ((), ()))


def kernel(
    n, kv_count, group,
    q_hbm, k_hbm, v_hbm, g_hbm, ids_ref,
    dq_hbm, dk_hbm, dv_hbm,
    q_ref, g_ref, kv, ids, own, bias, scores, prods, probs, grads, part, out_buf, in_buf,
    dq_ref, dkv_ref, fetch_sem, store_sem,
    kv_send, kv_recv, back_send, back_recv, ids_send, ids_recv,
):
    me = lax.axis_index("sp")
    odd = lax.rem(me, 2) == 1
    tokens = q_hbm.shape[0]
    span = SLOTS * tokens
    scale = HEAD_DIM ** (-0.5)
    up = me + 2 < n
    partner = jnp.where(odd, me - 1, me + 1)

    def kv_copy(c, src, dst, which, target):
        return pltpu.make_async_remote_copy(
            src_ref=kv.at[c, src],
            dst_ref=kv.at[c, dst],
            send_sem=kv_send.at[c, which],
            recv_sem=kv_recv.at[c, dst - 1],
            device_id={"sp": target},
            device_id_type=pl.DeviceIdType.MESH,
        )

    def back_copy(c, slot, target):
        return pltpu.make_async_remote_copy(
            src_ref=out_buf.at[c, slot - 1],
            dst_ref=in_buf.at[c, slot - 1],
            send_sem=back_send.at[c, slot - 1],
            recv_sem=back_recv.at[c, slot - 1],
            device_id={"sp": target},
            device_id_type=pl.DeviceIdType.MESH,
        )

    def ids_copy(d):
        return pltpu.make_async_remote_copy(
            src_ref=ids_ref,
            dst_ref=ids.at[d],
            send_sem=ids_send.at[d - 1],
            recv_sem=ids_recv.at[d - 1],
            device_id={"sp": me + d},
            device_id_type=pl.DeviceIdType.MESH,
        )

    barrier = pltpu.get_barrier_semaphore()
    for d in range(1, SLOTS):
        @pl.when(me >= d)
        def _():
            pl.semaphore_signal(
                barrier, inc=1, device_id={"sp": me - d}, device_id_type=pl.DeviceIdType.MESH
            )

        @pl.when(me + d < n)
        def _():
            pl.semaphore_signal(
                barrier, inc=1, device_id={"sp": me + d}, device_id_type=pl.DeviceIdType.MESH
            )

    def fetch(c, what):
        if what < 2:
            cols = pl.ds(pl.multiple_of(c * HEAD_DIM, HEAD_DIM), HEAD_DIM)
            return pltpu.make_async_copy(
                (k_hbm, v_hbm)[what].at[:, cols], kv.at[c, 0, what], fetch_sem.at[c, what]
            )
        width = group * HEAD_DIM
        cols = pl.ds(pl.multiple_of(c * width, width), width)
        source, target = ((q_hbm, q_ref), (g_hbm, g_ref))[what - 2]
        return pltpu.make_async_copy(source.at[:, cols], target.at[c], fetch_sem.at[c, what])

    def store(c, what):
        if what < 2:
            cols = pl.ds(pl.multiple_of(c * HEAD_DIM, HEAD_DIM), HEAD_DIM)
            source, target = dkv_ref.at[c, what], (dk_hbm, dv_hbm)[what].at[:, cols]
        else:
            width = group * HEAD_DIM
            cols = pl.ds(pl.multiple_of(c * width, width), width)
            source, target = dq_ref.at[c], dq_hbm.at[:, cols]
        return pltpu.make_async_copy(source, target, store_sem.at[c, what])

    def start_fetch(c, first):
        fetch(c, first).start()
        fetch(c, first + 1).start()
        return 0

    lax.fori_loop(0, kv_count, lambda c, _: start_fetch(c, 0), 0)
    lax.fori_loop(0, kv_count, lambda c, _: start_fetch(c, 2), 0)

    def fill(c, _):
        for d in range(1, SLOTS):
            @pl.when(me < d)
            def _():
                kv[c, d] = jnp.zeros((2, tokens, HEAD_DIM), kv.dtype)
        return 0

    lax.fori_loop(0, kv_count, fill, 0)
    ids[0] = ids_ref[...]
    for d in range(1, SLOTS):
        @pl.when(me < d)
        def _():
            ids[d] = jnp.full(ids_ref.shape, -1, jnp.int32)

    pl.semaphore_wait(barrier, jnp.minimum(me, REACH) + jnp.minimum(n - 1 - me, REACH))

    def send_own(c):
        fetch(c, 0).wait()
        fetch(c, 1).wait()

        @pl.when(up)
        def _():
            kv_copy(c, 0, 2, 0, me + 2).start()

        @pl.when(jnp.logical_not(odd))
        def _():
            kv_copy(c, 0, 1, 2, me + 1).start()

    for d in range(1, SLOTS):
        @pl.when(me + d < n)
        def _():
            ids_copy(d).start()

    ahead = min(2, kv_count)
    for c in range(ahead):
        send_own(c)

    for d in range(1, SLOTS):
        @pl.when(me >= d)
        def _():
            ids_copy(d).wait_recv()

    key_at = lax.broadcasted_iota(jnp.int32, (tokens, tokens), 0)
    query_at = lax.broadcasted_iota(jnp.int32, (tokens, tokens), 1)
    row = jnp.broadcast_to(ids[0, 0:1, :].astype(jnp.float32), (tokens, tokens))
    own[...] = (key_at <= query_at).astype(jnp.float32)

    def ids_of(d):
        return jnp.broadcast_to(ids[d, 0:1, :].astype(jnp.float32), (tokens, tokens)).T

    for d in range(REACH):
        col = jnp.where(own[...] > 0.0, ids_of(0), ids_of(REACH)) if d == 0 else ids_of(d)
        bias[d * tokens:(d + 1) * tokens, :] = jnp.where(col == row, 0.0, -1e30)

    def stack(ref, c, first, count):
        cols = [ref[c, :, (first + i) * HEAD_DIM:(first + i + 1) * HEAD_DIM] for i in range(count)]
        return jnp.concatenate(cols, axis=0)

    def fold(array, combine):
        rows = [array[8 * i:8 * (i + 1)] for i in range(array.shape[0] // 8)]
        while len(rows) > 1:
            rows = [combine(rows[i], rows[i + 1]) for i in range(0, len(rows), 2)]
        return rows[0]

    factor = scale * LOG2E
    tile = 64
    last = REACH * tokens

    def twice(array):
        return jnp.concatenate([array, array], axis=1)

    def merged(array, at):
        block = array[at:at + tile]
        if at < tokens:
            block = jnp.where(
                twice(own[at:at + tile, :]) > 0.0, block, array[last + at:last + at + tile]
            )
        return block

    def put(ref, at, lanes, block):
        if at < tokens:
            mine = twice(own[at:at + tile, :]) > 0.0
            ref[at:at + tile, lanes] = jnp.where(mine, block, 0.0).astype(jnp.bfloat16)
            ref[last + at:last + at + tile, lanes] = jnp.where(mine, 0.0, block).astype(
                jnp.bfloat16
            )
        else:
            ref[at:at + tile, lanes] = block.astype(jnp.bfloat16)

    def lanes_of(pair):
        return slice(pair * 2 * tokens, (pair + 1) * 2 * tokens)

    def score_pass(c, pair):
        keys = kv[c, :, 0].reshape(span, HEAD_DIM)
        q_pair = stack(q_ref, c, 2 * pair, 2)
        s_all = lax.dot_general(keys, q_pair, NT, preferred_element_type=jnp.float32)
        tops = []
        for at in range(0, last, tile):
            s = merged(s_all, at) + twice(bias[at:at + tile, :])
            scores[at:at + tile, lanes_of(pair)] = s
            tops.append(fold(s, jnp.maximum))
        return jnp.max(functools.reduce(jnp.maximum, tops), axis=0, keepdims=True) * factor

    def exp_pass(c, pair, top):
        lanes = lanes_of(pair)
        values = kv[c, :, 1].reshape(span, HEAD_DIM)
        g_pair = stack(g_ref, c, 2 * pair, 2)
        dp_all = lax.dot_general(values, g_pair, NT, preferred_element_type=jnp.float32)
        sums, dots = [], []
        for at in range(0, last, tile):
            e = jnp.exp2(scores[at:at + tile, lanes] * factor - top)
            dp = merged(dp_all, at)
            scores[at:at + tile, lanes] = e
            prods[at:at + tile, lanes] = dp
            sums.append(fold(e, jnp.add))
            dots.append(fold(e * dp, jnp.add))
        inverse = 1.0 / jnp.sum(functools.reduce(jnp.add, sums), axis=0, keepdims=True)
        delta = jnp.sum(functools.reduce(jnp.add, dots), axis=0, keepdims=True) * inverse
        return inverse, delta

    def grad_pass(pair, inverse, delta):
        lanes = lanes_of(pair)
        for at in range(0, last, tile):
            p = scores[at:at + tile, lanes] * inverse
            put(probs, at, lanes, p)
            put(grads, at, lanes, p * (prods[at:at + tile, lanes] - delta))

    def put_parts(c, which, array):
        for d in range(SLOTS):
            block = array[d * tokens:(d + 1) * tokens]
            if d <= 2:
                part[c, d, which] = block
            else:
                out_buf[c, d - 1, which] = block.astype(jnp.bfloat16)

    def value_products(c):
        dv = jnp.dot(probs[...], stack(g_ref, c, 0, group), preferred_element_type=jnp.float32)
        put_parts(c, 1, dv)

    def key_products(c):
        dk = jnp.dot(grads[...], stack(q_ref, c, 0, group), preferred_element_type=jnp.float32)
        put_parts(c, 0, scale * dk)

    def query_products(c):
        keys = kv[c, :, 0].reshape(span, HEAD_DIM)
        dq_t = scale * jnp.dot(keys.T, grads[...], preferred_element_type=jnp.float32)
        for h in range(group):
            dq_ref[c, :, h * HEAD_DIM:(h + 1) * HEAD_DIM] = (
                dq_t[:, h * tokens:(h + 1) * tokens].T.astype(jnp.bfloat16)
            )

    def compute(c, softmax, products):
        pairs = group // 2
        before = [value_products, key_products, query_products] if products else []
        tops, rest = {}, {}
        for at in range(pairs + 3):
            if softmax and at < pairs:
                tops[at] = score_pass(c, at)
            if before:
                before.pop(0)(c - 1)
            if softmax and 1 <= at <= pairs:
                rest[at - 1] = exp_pass(c, at - 1, tops[at - 1])
            if softmax and at >= 3:
                grad_pass(at - 3, *rest[at - 3])

    def within(c):
        return (c >= 0) & (c < kv_count)

    def step(t, _):
        c = t - 2

        @pl.when(within(t - 1) & (me >= 1))
        def _():
            kv_copy(t - 1, 0, 1, 2, me).wait_recv()

            @pl.when(up)
            def _():
                kv_copy(t - 1, 1, 3, 3, me + 2).start()

        @pl.when(within(t) & (me >= 2))
        def _():
            kv_copy(t, 0, 2, 0, me).wait_recv()

            @pl.when(odd)
            def _():
                kv_copy(t, 2, 1, 2, me - 1).start()

            @pl.when(up)
            def _():
                kv_copy(t, 2, 4, 1, me + 2).start()

        @pl.when(within(c))
        def _():
            @pl.when(me >= 3)
            def _():
                kv_copy(c, 1, 3, 3, me).wait_recv()

            @pl.when(me >= 4)
            def _():
                kv_copy(c, 2, 4, 1, me).wait_recv()

            fetch(c, 2).wait()
            fetch(c, 3).wait()

        @pl.when(c == 0)
        def _():
            compute(c, True, False)

        @pl.when((c >= 1) & (c < kv_count))
        def _():
            compute(c, True, True)

        @pl.when(c == kv_count)
        def _():
            compute(c, False, True)

        @pl.when(within(c - 1))
        def _():
            @pl.when(me >= 3)
            def _():
                back_copy(c - 1, 3, me - 2).start()

            @pl.when(me >= 4)
            def _():
                back_copy(c - 1, 4, me - 2).start()

            store(c - 1, 2).start()

        @pl.when(t + ahead < kv_count)
        def _():
            send_own(t + ahead)

        @pl.when(within(c - 3))
        def _():
            b = c - 3

            @pl.when(up & (me >= 1))
            def _():
                back_copy(b, 3, me).wait_recv()
                part[b, 1] += in_buf[b, 2].astype(jnp.float32)

            @pl.when(up & (me >= 2))
            def _():
                back_copy(b, 4, me).wait_recv()
                part[b, 2] += in_buf[b, 3].astype(jnp.float32)

            @pl.when(me >= 1)
            def _():
                out_buf[b, 0] = part[b, 1].astype(jnp.bfloat16)
                back_copy(b, 1, partner).start()

        @pl.when(within(c - 4))
        def _():
            b = c - 4

            @pl.when(odd & (me >= 3))
            def _():
                back_copy(b, 1, me).wait_recv()
                part[b, 2] += in_buf[b, 0].astype(jnp.float32)

            @pl.when(jnp.logical_not(odd))
            def _():
                back_copy(b, 1, me).wait_recv()
                part[b, 0] += in_buf[b, 0].astype(jnp.float32)

            @pl.when(me >= 2)
            def _():
                out_buf[b, 1] = part[b, 2].astype(jnp.bfloat16)
                back_copy(b, 2, me - 2).start()

        @pl.when(within(c - 6))
        def _():
            b = c - 6

            @pl.when(up)
            def _():
                back_copy(b, 2, me).wait_recv()
                part[b, 0] += in_buf[b, 1].astype(jnp.float32)

            dkv_ref[b] = part[b, 0].astype(jnp.bfloat16)
            store(b, 0).start()
            store(b, 1).start()

        return 0

    lax.fori_loop(0, kv_count + 8, step, 0)

    def drain(c, _):
        @pl.when(up)
        def _():
            kv_copy(c, 0, 2, 0, me).wait_send()

            @pl.when(me >= 2)
            def _():
                kv_copy(c, 2, 4, 1, me).wait_send()

            @pl.when(me >= 1)
            def _():
                kv_copy(c, 1, 3, 3, me).wait_send()

        @pl.when(jnp.logical_not(odd) | (me >= 3))
        def _():
            kv_copy(c, 0, 1, 2, me).wait_send()

        for slot in range(1, SLOTS):
            @pl.when(me >= slot)
            def _():
                back_copy(c, slot, me).wait_send()
        for what in range(3):
            store(c, what).wait()
        return 0

    lax.fori_loop(0, kv_count, drain, 0)
    for d in range(1, SLOTS):
        @pl.when(me + d < n)
        def _():
            ids_copy(d).wait_send()


def finish(dq_in, dk_in, dv_in, dq_out, dk_out, dv_out):
    dq_out[...] = dq_in[...]
    dk_out[...] = dk_in[...]
    dv_out[...] = dv_in[...]


def body(queries, key_heads, value_heads, out_grad, segment_ids):
    tokens, width = queries.shape
    kv_width = key_heads.shape[1]
    kv_count = kv_width // HEAD_DIM
    group = width // kv_width
    n = lax.axis_size("sp")
    assert -(-(MOST - 1) // tokens) == REACH and n % 2 == 0 and group % 2 == 0
    ids_rows = jnp.broadcast_to(segment_ids[None, :], (8, tokens))
    span = SLOTS * tokens
    vmem = pl.BlockSpec(memory_space=pltpu.VMEM)
    pairs = (kv_count, REACH, 2, tokens, HEAD_DIM)
    dma = pltpu.SemaphoreType.DMA
    elements = kv_count * group * tokens * span
    shapes = (
        jax.ShapeDtypeStruct((tokens, width), jnp.bfloat16),
        jax.ShapeDtypeStruct((tokens, kv_width), jnp.bfloat16),
        jax.ShapeDtypeStruct((tokens, kv_width), jnp.bfloat16),
    )
    anywhere = pl.BlockSpec(memory_space=pl.ANY)
    grads = pl.pallas_call(
        functools.partial(kernel, n, kv_count, group),
        out_shape=shapes,
        in_specs=[pl.BlockSpec(memory_space=pltpu.HBM)] * 4 + [vmem],
        out_specs=(anywhere, anywhere, anywhere),
        scratch_shapes=[
            pltpu.VMEM((kv_count, tokens, group * HEAD_DIM), jnp.bfloat16),
            pltpu.VMEM((kv_count, tokens, group * HEAD_DIM), jnp.bfloat16),
            pltpu.VMEM((kv_count, SLOTS, 2, tokens, HEAD_DIM), jnp.bfloat16),
            pltpu.VMEM((SLOTS, 8, tokens), jnp.int32),
            pltpu.VMEM((tokens, tokens), jnp.float32),
            pltpu.VMEM((REACH * tokens, tokens), jnp.float32),
            pltpu.VMEM((REACH * tokens, group * tokens), jnp.float32),
            pltpu.VMEM((REACH * tokens, group * tokens), jnp.float32),
            pltpu.VMEM((span, group * tokens), jnp.bfloat16),
            pltpu.VMEM((span, group * tokens), jnp.bfloat16),
            pltpu.VMEM((kv_count, 3, 2, tokens, HEAD_DIM), jnp.float32),
            pltpu.VMEM(pairs, jnp.bfloat16),
            pltpu.VMEM(pairs, jnp.bfloat16),
            pltpu.VMEM((kv_count, tokens, group * HEAD_DIM), jnp.bfloat16),
            pltpu.VMEM((kv_count, 2, tokens, HEAD_DIM), jnp.bfloat16),
            dma((kv_count, 4)),
            dma((kv_count, 3)),
            dma((kv_count, 4)),
            dma((kv_count, REACH)),
            dma((kv_count, REACH)),
            dma((kv_count, REACH)),
            dma((REACH,)),
            dma((REACH,)),
        ],
        compiler_params=pltpu.CompilerParams(
            collective_id=0, has_side_effects=True, vmem_limit_bytes=61 * 1024 * 1024
        ),
        cost_estimate=pl.CostEstimate(
            flops=10 * elements * HEAD_DIM,
            bytes_accessed=6 * tokens * width + 8 * tokens * kv_width,
            transcendentals=elements,
        ),
    )(queries, key_heads, value_heads, out_grad, ids_rows)
    blocks = tuple(
        pl.BlockSpec((tokens // 4, shape.shape[1]), lambda i: (i, 0)) for shape in shapes
    )
    return pl.pallas_call(
        finish,
        out_shape=shapes,
        grid=(4,),
        in_specs=list(blocks),
        out_specs=blocks,
        compiler_params=pltpu.CompilerParams(vmem_limit_bytes=61 * 1024 * 1024),
    )(*grads)


def solution(mesh):
    rows = P(("dp", "sp"), None)
    return jax.shard_map(
        body,
        mesh=mesh,
        in_specs=(rows, rows, rows, rows, P(("dp", "sp"))),
        out_specs=(rows, rows, rows),
        check_vma=False,
    )
```

```python
import functools

import jax
import jax.numpy as jnp
from jax import lax
from jax.experimental import pallas as pl
from jax.experimental.pallas import tpu as pltpu
from jax.sharding import PartitionSpec as P

HEAD_DIM = 128
MOST = 512
REACH = 4
SLOTS = REACH + 1
LOG2E = 1.4426950408889634
NT = (((1,), (1,)), ((), ()))


def kernel(
    n, kv_count, group,
    q_hbm, k_hbm, v_hbm, g_hbm, ids_ref,
    dq_hbm, dk_hbm, dv_hbm,
    q_ref, g_ref, kv, ids, own, bias, scores, prods, probs, grads, part, out_buf, in_buf,
    dq_ref, dkv_ref, fetch_sem, store_sem,
    kv_send, kv_recv, back_send, back_recv, ids_send, ids_recv,
):
    me = lax.axis_index("sp")
    odd = lax.rem(me, 2) == 1
    tokens = q_hbm.shape[0]
    span = SLOTS * tokens
    scale = HEAD_DIM ** (-0.5)
    up = me + 2 < n
    partner = jnp.where(odd, me - 1, me + 1)

    def kv_copy(c, src, dst, which, target):
        return pltpu.make_async_remote_copy(
            src_ref=kv.at[c, src],
            dst_ref=kv.at[c, dst],
            send_sem=kv_send.at[c, which],
            recv_sem=kv_recv.at[c, dst - 1],
            device_id={"sp": target},
            device_id_type=pl.DeviceIdType.MESH,
        )

    def back_copy(c, slot, target):
        return pltpu.make_async_remote_copy(
            src_ref=out_buf.at[c, slot - 1],
            dst_ref=in_buf.at[c, slot - 1],
            send_sem=back_send.at[c, slot - 1],
            recv_sem=back_recv.at[c, slot - 1],
            device_id={"sp": target},
            device_id_type=pl.DeviceIdType.MESH,
        )

    def ids_copy(d):
        return pltpu.make_async_remote_copy(
            src_ref=ids_ref,
            dst_ref=ids.at[d],
            send_sem=ids_send.at[d - 1],
            recv_sem=ids_recv.at[d - 1],
            device_id={"sp": me + d},
            device_id_type=pl.DeviceIdType.MESH,
        )

    barrier = pltpu.get_barrier_semaphore()
    for d in range(1, SLOTS):
        @pl.when(me >= d)
        def _():
            pl.semaphore_signal(
                barrier, inc=1, device_id={"sp": me - d}, device_id_type=pl.DeviceIdType.MESH
            )

        @pl.when(me + d < n)
        def _():
            pl.semaphore_signal(
                barrier, inc=1, device_id={"sp": me + d}, device_id_type=pl.DeviceIdType.MESH
            )

    def fetch(c, what):
        if what < 2:
            cols = pl.ds(pl.multiple_of(c * HEAD_DIM, HEAD_DIM), HEAD_DIM)
            return pltpu.make_async_copy(
                (k_hbm, v_hbm)[what].at[:, cols], kv.at[c, 0, what], fetch_sem.at[c, what]
            )
        width = group * HEAD_DIM
        cols = pl.ds(pl.multiple_of(c * width, width), width)
        source, target = ((q_hbm, q_ref), (g_hbm, g_ref))[what - 2]
        return pltpu.make_async_copy(source.at[:, cols], target.at[c], fetch_sem.at[c, what])

    def store(c, what):
        if what < 2:
            cols = pl.ds(pl.multiple_of(c * HEAD_DIM, HEAD_DIM), HEAD_DIM)
            source, target = dkv_ref.at[c, what], (dk_hbm, dv_hbm)[what].at[:, cols]
        else:
            width = group * HEAD_DIM
            cols = pl.ds(pl.multiple_of(c * width, width), width)
            source, target = dq_ref.at[c], dq_hbm.at[:, cols]
        return pltpu.make_async_copy(source, target, store_sem.at[c, what])

    def start_fetch(c, first):
        fetch(c, first).start()
        fetch(c, first + 1).start()
        return 0

    lax.fori_loop(0, kv_count, lambda c, _: start_fetch(c, 0), 0)
    lax.fori_loop(0, kv_count, lambda c, _: start_fetch(c, 2), 0)

    def fill(c, _):
        for d in range(1, SLOTS):
            @pl.when(me < d)
            def _():
                kv[c, d] = jnp.zeros((2, tokens, HEAD_DIM), kv.dtype)
        return 0

    lax.fori_loop(0, kv_count, fill, 0)
    ids[0] = ids_ref[...]
    for d in range(1, SLOTS):
        @pl.when(me < d)
        def _():
            ids[d] = jnp.full(ids_ref.shape, -1, jnp.int32)

    pl.semaphore_wait(barrier, jnp.minimum(me, REACH) + jnp.minimum(n - 1 - me, REACH))

    def send_own(c):
        fetch(c, 0).wait()
        fetch(c, 1).wait()

        @pl.when(up)
        def _():
            kv_copy(c, 0, 2, 0, me + 2).start()

        @pl.when(jnp.logical_not(odd))
        def _():
            kv_copy(c, 0, 1, 2, me + 1).start()

    for d in range(1, SLOTS):
        @pl.when(me + d < n)
        def _():
            ids_copy(d).start()

    ahead = min(2, kv_count)
    for c in range(ahead):
        send_own(c)

    for d in range(1, SLOTS):
        @pl.when(me >= d)
        def _():
            ids_copy(d).wait_recv()

    key_at = lax.broadcasted_iota(jnp.int32, (tokens, tokens), 0)
    query_at = lax.broadcasted_iota(jnp.int32, (tokens, tokens), 1)
    row = jnp.broadcast_to(ids[0, 0:1, :].astype(jnp.float32), (tokens, tokens))
    own[...] = (key_at <= query_at).astype(jnp.float32)

    def ids_of(d):
        return jnp.broadcast_to(ids[d, 0:1, :].astype(jnp.float32), (tokens, tokens)).T

    for d in range(REACH):
        col = jnp.where(own[...] > 0.0, ids_of(0), ids_of(REACH)) if d == 0 else ids_of(d)
        bias[d * tokens:(d + 1) * tokens, :] = jnp.where(col == row, 0.0, -1e30)

    def stack(ref, c, first, count):
        cols = [ref[c, :, (first + i) * HEAD_DIM:(first + i + 1) * HEAD_DIM] for i in range(count)]
        return jnp.concatenate(cols, axis=0)

    def fold(array, combine):
        rows = [array[8 * i:8 * (i + 1)] for i in range(array.shape[0] // 8)]
        while len(rows) > 1:
            rows = [combine(rows[i], rows[i + 1]) for i in range(0, len(rows), 2)]
        return rows[0]

    factor = scale * LOG2E
    tile = 64
    last = REACH * tokens

    def twice(array):
        return jnp.concatenate([array, array], axis=1)

    def merged(array, at):
        block = array[at:at + tile]
        if at < tokens:
            block = jnp.where(
                twice(own[at:at + tile, :]) > 0.0, block, array[last + at:last + at + tile]
            )
        return block

    def put(ref, at, lanes, block):
        if at < tokens:
            mine = twice(own[at:at + tile, :]) > 0.0
            ref[at:at + tile, lanes] = jnp.where(mine, block, 0.0).astype(jnp.bfloat16)
            ref[last + at:last + at + tile, lanes] = jnp.where(mine, 0.0, block).astype(
                jnp.bfloat16
            )
        else:
            ref[at:at + tile, lanes] = block.astype(jnp.bfloat16)

    def lanes_of(pair):
        return slice(pair * 2 * tokens, (pair + 1) * 2 * tokens)

    def score_pass(c, pair):
        keys = kv[c, :, 0].reshape(span, HEAD_DIM)
        q_pair = stack(q_ref, c, 2 * pair, 2)
        s_all = lax.dot_general(keys, q_pair, NT, preferred_element_type=jnp.float32)
        tops = []
        for at in range(0, last, tile):
            s = merged(s_all, at) + twice(bias[at:at + tile, :])
            scores[at:at + tile, lanes_of(pair)] = s
            tops.append(fold(s, jnp.maximum))
        return jnp.max(functools.reduce(jnp.maximum, tops), axis=0, keepdims=True) * factor

    def exp_pass(c, pair, top):
        lanes = lanes_of(pair)
        values = kv[c, :, 1].reshape(span, HEAD_DIM)
        g_pair = stack(g_ref, c, 2 * pair, 2)
        dp_all = lax.dot_general(values, g_pair, NT, preferred_element_type=jnp.float32)
        sums, dots = [], []
        for at in range(0, last, tile):
            e = jnp.exp2(scores[at:at + tile, lanes] * factor - top)
            dp = merged(dp_all, at)
            scores[at:at + tile, lanes] = e
            prods[at:at + tile, lanes] = dp
            sums.append(fold(e, jnp.add))
            dots.append(fold(e * dp, jnp.add))
        inverse = 1.0 / jnp.sum(functools.reduce(jnp.add, sums), axis=0, keepdims=True)
        delta = jnp.sum(functools.reduce(jnp.add, dots), axis=0, keepdims=True) * inverse
        return inverse, delta

    def grad_pass(pair, inverse, delta):
        lanes = lanes_of(pair)
        for at in range(0, last, tile):
            p = scores[at:at + tile, lanes] * inverse
            put(probs, at, lanes, p)
            put(grads, at, lanes, p * (prods[at:at + tile, lanes] - delta))

    def first_half(c):
        fetch(c, 2).wait()
        fetch(c, 3).wait()
        pairs = group // 2
        tops, rest = {}, {}
        for at in range(pairs + 2):
            if at < pairs:
                tops[at] = score_pass(c, at)
            if 1 <= at <= pairs:
                rest[at - 1] = exp_pass(c, at - 1, tops[at - 1])
            if at >= 2:
                grad_pass(at - 2, *rest[at - 2])

    def second_half(c):
        dv = jnp.dot(probs[...], stack(g_ref, c, 0, group), preferred_element_type=jnp.float32)
        dk = scale * jnp.dot(
            grads[...], stack(q_ref, c, 0, group), preferred_element_type=jnp.float32
        )
        for d in range(SLOTS):
            for which, array in ((0, dk), (1, dv)):
                block = array[d * tokens:(d + 1) * tokens]
                if d <= 2:
                    part[c, d, which] = block
                else:
                    out_buf[c, d - 1, which] = block.astype(jnp.bfloat16)

        @pl.when(me >= 3)
        def _():
            back_copy(c, 3, me - 2).start()

        @pl.when(me >= 4)
        def _():
            back_copy(c, 4, me - 2).start()

        keys = kv[c, :, 0].reshape(span, HEAD_DIM)
        dq_t = scale * jnp.dot(keys.T, grads[...], preferred_element_type=jnp.float32)
        for h in range(group):
            dq_ref[c, :, h * HEAD_DIM:(h + 1) * HEAD_DIM] = (
                dq_t[:, h * tokens:(h + 1) * tokens].T.astype(jnp.bfloat16)
            )
        store(c, 2).start()

    def within(c):
        return (c >= 0) & (c < kv_count)

    def step(t, _):
        c = t - 2

        @pl.when(within(t - 1) & (me >= 1))
        def _():
            kv_copy(t - 1, 0, 1, 2, me).wait_recv()

            @pl.when(up)
            def _():
                kv_copy(t - 1, 1, 3, 3, me + 2).start()

        @pl.when(within(t) & (me >= 2))
        def _():
            kv_copy(t, 0, 2, 0, me).wait_recv()

            @pl.when(odd)
            def _():
                kv_copy(t, 2, 1, 2, me - 1).start()

            @pl.when(up)
            def _():
                kv_copy(t, 2, 4, 1, me + 2).start()

        @pl.when(within(c))
        def _():
            @pl.when(me >= 3)
            def _():
                kv_copy(c, 1, 3, 3, me).wait_recv()

            @pl.when(me >= 4)
            def _():
                kv_copy(c, 2, 4, 1, me).wait_recv()

            first_half(c)

        @pl.when(t + ahead < kv_count)
        def _():
            send_own(t + ahead)

        @pl.when(within(c - 2))
        def _():
            b = c - 2

            @pl.when(up & (me >= 1))
            def _():
                back_copy(b, 3, me).wait_recv()
                part[b, 1] += in_buf[b, 2].astype(jnp.float32)

            @pl.when(up & (me >= 2))
            def _():
                back_copy(b, 4, me).wait_recv()
                part[b, 2] += in_buf[b, 3].astype(jnp.float32)

            @pl.when(me >= 1)
            def _():
                out_buf[b, 0] = part[b, 1].astype(jnp.bfloat16)
                back_copy(b, 1, partner).start()

        @pl.when(within(c - 3))
        def _():
            b = c - 3

            @pl.when(odd & (me >= 3))
            def _():
                back_copy(b, 1, me).wait_recv()
                part[b, 2] += in_buf[b, 0].astype(jnp.float32)

            @pl.when(jnp.logical_not(odd))
            def _():
                back_copy(b, 1, me).wait_recv()
                part[b, 0] += in_buf[b, 0].astype(jnp.float32)

            @pl.when(me >= 2)
            def _():
                out_buf[b, 1] = part[b, 2].astype(jnp.bfloat16)
                back_copy(b, 2, me - 2).start()

        @pl.when(within(c - 5))
        def _():
            b = c - 5

            @pl.when(up)
            def _():
                back_copy(b, 2, me).wait_recv()
                part[b, 0] += in_buf[b, 1].astype(jnp.float32)

            dkv_ref[b] = part[b, 0].astype(jnp.bfloat16)
            store(b, 0).start()
            store(b, 1).start()

        @pl.when(within(c))
        def _():
            second_half(c)

        return 0

    lax.fori_loop(0, kv_count + 7, step, 0)

    def drain(c, _):
        @pl.when(up)
        def _():
            kv_copy(c, 0, 2, 0, me).wait_send()

            @pl.when(me >= 2)
            def _():
                kv_copy(c, 2, 4, 1, me).wait_send()

            @pl.when(me >= 1)
            def _():
                kv_copy(c, 1, 3, 3, me).wait_send()

        @pl.when(jnp.logical_not(odd) | (me >= 3))
        def _():
            kv_copy(c, 0, 1, 2, me).wait_send()

        for slot in range(1, SLOTS):
            @pl.when(me >= slot)
            def _():
                back_copy(c, slot, me).wait_send()
        for what in range(3):
            store(c, what).wait()
        return 0

    lax.fori_loop(0, kv_count, drain, 0)
    for d in range(1, SLOTS):
        @pl.when(me + d < n)
        def _():
            ids_copy(d).wait_send()


def finish(dq_in, dk_in, dv_in, dq_out, dk_out, dv_out, dq_held, dk_held, dv_held, come, go):
    tokens = dq_in.shape[0]
    part = tokens // 4
    moves = [(dq_in, dq_held, dq_out, pl.ds(i * part, part)) for i in range(4)]
    moves.append((dk_in, dk_held, dk_out, pl.ds(0, tokens)))
    moves.append((dv_in, dv_held, dv_out, pl.ds(0, tokens)))
    first = [
        pltpu.make_async_copy(source.at[rows], held.at[rows], come.at[i])
        for i, (source, held, _, rows) in enumerate(moves)
    ]
    second = [
        pltpu.make_async_copy(held.at[rows], target.at[rows], go.at[i])
        for i, (_, held, target, rows) in enumerate(moves)
    ]
    for copy in first:
        copy.start()
    for before, after in zip(first, second):
        before.wait()
        after.start()
    for copy in second:
        copy.wait()


def body(queries, key_heads, value_heads, out_grad, segment_ids):
    tokens, width = queries.shape
    kv_width = key_heads.shape[1]
    kv_count = kv_width // HEAD_DIM
    group = width // kv_width
    n = lax.axis_size("sp")
    assert -(-(MOST - 1) // tokens) == REACH and n % 2 == 0 and group % 2 == 0
    ids_rows = segment_ids.reshape(1, tokens)
    span = SLOTS * tokens
    vmem = pl.BlockSpec(memory_space=pltpu.VMEM)
    pairs = (kv_count, REACH, 2, tokens, HEAD_DIM)
    dma = pltpu.SemaphoreType.DMA
    elements = kv_count * group * tokens * span
    shapes = (
        jax.ShapeDtypeStruct((tokens, width), jnp.bfloat16),
        jax.ShapeDtypeStruct((tokens, kv_width), jnp.bfloat16),
        jax.ShapeDtypeStruct((tokens, kv_width), jnp.bfloat16),
    )
    anywhere = pl.BlockSpec(memory_space=pl.ANY)
    grads = pl.pallas_call(
        functools.partial(kernel, n, kv_count, group),
        out_shape=shapes,
        in_specs=[pl.BlockSpec(memory_space=pltpu.HBM)] * 4 + [vmem],
        out_specs=(anywhere, anywhere, anywhere),
        scratch_shapes=[
            pltpu.VMEM((kv_count, tokens, group * HEAD_DIM), jnp.bfloat16),
            pltpu.VMEM((kv_count, tokens, group * HEAD_DIM), jnp.bfloat16),
            pltpu.VMEM((kv_count, SLOTS, 2, tokens, HEAD_DIM), jnp.bfloat16),
            pltpu.VMEM((SLOTS, 1, tokens), jnp.int32),
            pltpu.VMEM((tokens, tokens), jnp.float32),
            pltpu.VMEM((REACH * tokens, tokens), jnp.float32),
            pltpu.VMEM((REACH * tokens, group * tokens), jnp.float32),
            pltpu.VMEM((REACH * tokens, group * tokens), jnp.float32),
            pltpu.VMEM((span, group * tokens), jnp.bfloat16),
            pltpu.VMEM((span, group * tokens), jnp.bfloat16),
            pltpu.VMEM((kv_count, 3, 2, tokens, HEAD_DIM), jnp.float32),
            pltpu.VMEM(pairs, jnp.bfloat16),
            pltpu.VMEM(pairs, jnp.bfloat16),
            pltpu.VMEM((kv_count, tokens, group * HEAD_DIM), jnp.bfloat16),
            pltpu.VMEM((kv_count, 2, tokens, HEAD_DIM), jnp.bfloat16),
            dma((kv_count, 4)),
            dma((kv_count, 3)),
            dma((kv_count, 4)),
            dma((kv_count, REACH)),
            dma((kv_count, REACH)),
            dma((kv_count, REACH)),
            dma((REACH,)),
            dma((REACH,)),
        ],
        compiler_params=pltpu.CompilerParams(
            collective_id=0, has_side_effects=True, vmem_limit_bytes=61 * 1024 * 1024
        ),
        cost_estimate=pl.CostEstimate(
            flops=10 * elements * HEAD_DIM,
            bytes_accessed=6 * tokens * width + 8 * tokens * kv_width,
            transcendentals=elements,
        ),
    )(queries, key_heads, value_heads, out_grad, ids_rows)
    return pl.pallas_call(
        finish,
        out_shape=shapes,
        in_specs=[anywhere] * 3,
        out_specs=(anywhere, anywhere, anywhere),
        scratch_shapes=[pltpu.VMEM(shape.shape, jnp.bfloat16) for shape in shapes]
        + [dma((6,)), dma((6,))],
        compiler_params=pltpu.CompilerParams(vmem_limit_bytes=61 * 1024 * 1024),
    )(*grads)


def solution(mesh):
    rows = P(("dp", "sp"), None)
    return jax.shard_map(
        body,
        mesh=mesh,
        in_specs=(rows, rows, rows, rows, P(("dp", "sp"))),
        out_specs=(rows, rows, rows),
        check_vma=False,
    )
```

```python
import functools

import jax
import jax.numpy as jnp
from jax import lax
from jax.experimental import pallas as pl
from jax.experimental.pallas import tpu as pltpu
from jax.sharding import PartitionSpec as P

HEAD_DIM = 128
MOST = 512
REACH = 4
SLOTS = REACH + 1
LOG2E = 1.4426950408889634
NT = (((1,), (1,)), ((), ()))


def kernel(
    n, kv_count, group,
    q_hbm, k_hbm, v_hbm, g_hbm, ids_ref,
    dq_hbm, dk_hbm, dv_hbm,
    q_ref, g_ref, kv, ids, own, bias, scores, prods, probs, grads, part, out_buf, in_buf,
    dq_ref, dkv_ref, fetch_sem, store_sem,
    kv_send, kv_recv, back_send, back_recv, ids_send, ids_recv,
):
    me = lax.axis_index("sp")
    odd = lax.rem(me, 2) == 1
    tokens = q_hbm.shape[0]
    span = SLOTS * tokens
    scale = HEAD_DIM ** (-0.5)
    up = me + 2 < n
    partner = jnp.where(odd, me - 1, me + 1)

    def kv_copy(c, src, dst, which, target):
        return pltpu.make_async_remote_copy(
            src_ref=kv.at[c, src],
            dst_ref=kv.at[c, dst],
            send_sem=kv_send.at[c, which],
            recv_sem=kv_recv.at[c, dst - 1],
            device_id={"sp": target},
            device_id_type=pl.DeviceIdType.MESH,
        )

    def back_copy(c, slot, target):
        return pltpu.make_async_remote_copy(
            src_ref=out_buf.at[c, slot - 1],
            dst_ref=in_buf.at[c, slot - 1],
            send_sem=back_send.at[c, slot - 1],
            recv_sem=back_recv.at[c, slot - 1],
            device_id={"sp": target},
            device_id_type=pl.DeviceIdType.MESH,
        )

    def ids_copy(d):
        return pltpu.make_async_remote_copy(
            src_ref=ids_ref,
            dst_ref=ids.at[d],
            send_sem=ids_send.at[d - 1],
            recv_sem=ids_recv.at[d - 1],
            device_id={"sp": me + d},
            device_id_type=pl.DeviceIdType.MESH,
        )

    barrier = pltpu.get_barrier_semaphore()
    for d in range(1, SLOTS):
        @pl.when(me >= d)
        def _():
            pl.semaphore_signal(
                barrier, inc=1, device_id={"sp": me - d}, device_id_type=pl.DeviceIdType.MESH
            )

        @pl.when(me + d < n)
        def _():
            pl.semaphore_signal(
                barrier, inc=1, device_id={"sp": me + d}, device_id_type=pl.DeviceIdType.MESH
            )

    def fetch(c, what):
        if what < 2:
            cols = pl.ds(pl.multiple_of(c * HEAD_DIM, HEAD_DIM), HEAD_DIM)
            return pltpu.make_async_copy(
                (k_hbm, v_hbm)[what].at[:, cols], kv.at[c, 0, what], fetch_sem.at[c, what]
            )
        width = group * HEAD_DIM
        cols = pl.ds(pl.multiple_of(c * width, width), width)
        source, target = ((q_hbm, q_ref), (g_hbm, g_ref))[what - 2]
        return pltpu.make_async_copy(source.at[:, cols], target.at[c], fetch_sem.at[c, what])

    def store(c, what):
        if what < 2:
            cols = pl.ds(pl.multiple_of(c * HEAD_DIM, HEAD_DIM), HEAD_DIM)
            source, target = dkv_ref.at[c, what], (dk_hbm, dv_hbm)[what].at[:, cols]
        else:
            width = group * HEAD_DIM
            cols = pl.ds(pl.multiple_of(c * width, width), width)
            source, target = dq_ref.at[c], dq_hbm.at[:, cols]
        return pltpu.make_async_copy(source, target, store_sem.at[c, what])

    def start_fetch(c, first):
        fetch(c, first).start()
        fetch(c, first + 1).start()
        return 0

    lax.fori_loop(0, kv_count, lambda c, _: start_fetch(c, 0), 0)
    lax.fori_loop(0, kv_count, lambda c, _: start_fetch(c, 2), 0)

    def fill(c, _):
        for d in range(1, SLOTS):
            @pl.when(me < d)
            def _():
                kv[c, d] = jnp.zeros((2, tokens, HEAD_DIM), kv.dtype)
        return 0

    lax.fori_loop(0, kv_count, fill, 0)
    ids[0] = ids_ref[...]
    for d in range(1, SLOTS):
        @pl.when(me < d)
        def _():
            ids[d] = jnp.full(ids_ref.shape, -1, jnp.int32)

    pl.semaphore_wait(barrier, jnp.minimum(me, REACH) + jnp.minimum(n - 1 - me, REACH))

    def send_own(c):
        fetch(c, 0).wait()
        fetch(c, 1).wait()

        @pl.when(up)
        def _():
            kv_copy(c, 0, 2, 0, me + 2).start()

        @pl.when(jnp.logical_not(odd))
        def _():
            kv_copy(c, 0, 1, 2, me + 1).start()

    for d in range(1, SLOTS):
        @pl.when(me + d < n)
        def _():
            ids_copy(d).start()

    ahead = min(3, kv_count)
    for c in range(ahead):
        send_own(c)

    for d in range(1, SLOTS):
        @pl.when(me >= d)
        def _():
            ids_copy(d).wait_recv()

    key_at = lax.broadcasted_iota(jnp.int32, (tokens, tokens), 0)
    query_at = lax.broadcasted_iota(jnp.int32, (tokens, tokens), 1)
    row = jnp.broadcast_to(ids[0, 0:1, :].astype(jnp.float32), (tokens, tokens))
    own[...] = (key_at <= query_at).astype(jnp.float32)

    def ids_of(d):
        return jnp.broadcast_to(ids[d, 0:1, :].astype(jnp.float32), (tokens, tokens)).T

    for d in range(REACH):
        col = jnp.where(own[...] > 0.0, ids_of(0), ids_of(REACH)) if d == 0 else ids_of(d)
        bias[d * tokens:(d + 1) * tokens, :] = jnp.where(col == row, 0.0, -1e30)

    def stack(ref, c, first, count):
        cols = [ref[c, :, (first + i) * HEAD_DIM:(first + i + 1) * HEAD_DIM] for i in range(count)]
        return jnp.concatenate(cols, axis=0)

    def fold(array, combine):
        rows = [array[8 * i:8 * (i + 1)] for i in range(array.shape[0] // 8)]
        while len(rows) > 1:
            rows = [combine(rows[i], rows[i + 1]) for i in range(0, len(rows), 2)]
        return rows[0]

    factor = scale * LOG2E
    tile = 64
    last = REACH * tokens

    def twice(array):
        return jnp.concatenate([array, array], axis=1)

    def merged(array, at):
        block = array[at:at + tile]
        if at < tokens:
            block = jnp.where(
                twice(own[at:at + tile, :]) > 0.0, block, array[last + at:last + at + tile]
            )
        return block

    def put(ref, at, lanes, block):
        if at < tokens:
            mine = twice(own[at:at + tile, :]) > 0.0
            ref[at:at + tile, lanes] = jnp.where(mine, block, 0.0).astype(jnp.bfloat16)
            ref[last + at:last + at + tile, lanes] = jnp.where(mine, 0.0, block).astype(
                jnp.bfloat16
            )
        else:
            ref[at:at + tile, lanes] = block.astype(jnp.bfloat16)

    def lanes_of(pair):
        return slice(pair * 2 * tokens, (pair + 1) * 2 * tokens)

    def score_pass(c, pair):
        keys = kv[c, :, 0].reshape(span, HEAD_DIM)
        q_pair = stack(q_ref, c, 2 * pair, 2)
        s_all = lax.dot_general(keys, q_pair, NT, preferred_element_type=jnp.float32)
        tops = []
        for at in range(0, last, tile):
            s = merged(s_all, at) + twice(bias[at:at + tile, :])
            scores[at:at + tile, lanes_of(pair)] = s
            tops.append(fold(s, jnp.maximum))
        return jnp.max(functools.reduce(jnp.maximum, tops), axis=0, keepdims=True) * factor

    def exp_pass(c, pair, top):
        lanes = lanes_of(pair)
        values = kv[c, :, 1].reshape(span, HEAD_DIM)
        g_pair = stack(g_ref, c, 2 * pair, 2)
        dp_all = lax.dot_general(values, g_pair, NT, preferred_element_type=jnp.float32)
        sums, dots = [], []
        for at in range(0, last, tile):
            e = jnp.exp2(scores[at:at + tile, lanes] * factor - top)
            dp = merged(dp_all, at)
            scores[at:at + tile, lanes] = e
            prods[at:at + tile, lanes] = dp
            sums.append(fold(e, jnp.add))
            dots.append(fold(e * dp, jnp.add))
        inverse = 1.0 / jnp.sum(functools.reduce(jnp.add, sums), axis=0, keepdims=True)
        delta = jnp.sum(functools.reduce(jnp.add, dots), axis=0, keepdims=True) * inverse
        return inverse, delta

    def grad_pass(pair, inverse, delta):
        lanes = lanes_of(pair)
        for at in range(0, last, tile):
            p = scores[at:at + tile, lanes] * inverse
            put(probs, at, lanes, p)
            put(grads, at, lanes, p * (prods[at:at + tile, lanes] - delta))

    def first_half(c):
        fetch(c, 2).wait()
        fetch(c, 3).wait()
        pairs = group // 2
        tops, rest = {}, {}
        for at in range(pairs + 2):
            if at < pairs:
                tops[at] = score_pass(c, at)
            if 1 <= at <= pairs:
                rest[at - 1] = exp_pass(c, at - 1, tops[at - 1])
            if at >= 2:
                grad_pass(at - 2, *rest[at - 2])

    def second_half(c):
        dv = jnp.dot(probs[...], stack(g_ref, c, 0, group), preferred_element_type=jnp.float32)
        dk = scale * jnp.dot(
            grads[...], stack(q_ref, c, 0, group), preferred_element_type=jnp.float32
        )
        for d in range(SLOTS):
            for which, array in ((0, dk), (1, dv)):
                block = array[d * tokens:(d + 1) * tokens]
                if d <= 2:
                    part[c, d, which] = block
                else:
                    out_buf[c, d - 1, which] = block.astype(jnp.bfloat16)

        @pl.when(me >= 3)
        def _():
            back_copy(c, 3, me - 2).start()

        @pl.when(me >= 4)
        def _():
            back_copy(c, 4, me - 2).start()

        keys = kv[c, :, 0].reshape(span, HEAD_DIM)
        dq_t = scale * jnp.dot(keys.T, grads[...], preferred_element_type=jnp.float32)
        for h in range(group):
            dq_ref[c, :, h * HEAD_DIM:(h + 1) * HEAD_DIM] = (
                dq_t[:, h * tokens:(h + 1) * tokens].T.astype(jnp.bfloat16)
            )
        store(c, 2).start()

    def within(c):
        return (c >= 0) & (c < kv_count)

    def step(t, _):
        c = t - 2

        @pl.when(within(t - 1) & (me >= 1))
        def _():
            kv_copy(t - 1, 0, 1, 2, me).wait_recv()

            @pl.when(up)
            def _():
                kv_copy(t - 1, 1, 3, 3, me + 2).start()

        @pl.when(within(t) & (me >= 2))
        def _():
            kv_copy(t, 0, 2, 0, me).wait_recv()

            @pl.when(odd)
            def _():
                kv_copy(t, 2, 1, 2, me - 1).start()

            @pl.when(up)
            def _():
                kv_copy(t, 2, 4, 1, me + 2).start()

        @pl.when(within(c))
        def _():
            @pl.when(me >= 3)
            def _():
                kv_copy(c, 1, 3, 3, me).wait_recv()

            @pl.when(me >= 4)
            def _():
                kv_copy(c, 2, 4, 1, me).wait_recv()

            first_half(c)

        @pl.when(t + ahead < kv_count)
        def _():
            send_own(t + ahead)

        @pl.when(within(c - 2))
        def _():
            b = c - 2

            @pl.when(up & (me >= 1))
            def _():
                back_copy(b, 3, me).wait_recv()
                part[b, 1] += in_buf[b, 2].astype(jnp.float32)

            @pl.when(up & (me >= 2))
            def _():
                back_copy(b, 4, me).wait_recv()
                part[b, 2] += in_buf[b, 3].astype(jnp.float32)

            @pl.when(me >= 1)
            def _():
                out_buf[b, 0] = part[b, 1].astype(jnp.bfloat16)
                back_copy(b, 1, partner).start()

        @pl.when(within(c - 3))
        def _():
            b = c - 3

            @pl.when(odd & (me >= 3))
            def _():
                back_copy(b, 1, me).wait_recv()
                part[b, 2] += in_buf[b, 0].astype(jnp.float32)

            @pl.when(jnp.logical_not(odd))
            def _():
                back_copy(b, 1, me).wait_recv()
                part[b, 0] += in_buf[b, 0].astype(jnp.float32)

            @pl.when(me >= 2)
            def _():
                out_buf[b, 1] = part[b, 2].astype(jnp.bfloat16)
                back_copy(b, 2, me - 2).start()

        @pl.when(within(c - 5))
        def _():
            b = c - 5

            @pl.when(up)
            def _():
                back_copy(b, 2, me).wait_recv()
                part[b, 0] += in_buf[b, 1].astype(jnp.float32)

            dkv_ref[b] = part[b, 0].astype(jnp.bfloat16)
            store(b, 0).start()
            store(b, 1).start()

        @pl.when(within(c))
        def _():
            second_half(c)

        return 0

    lax.fori_loop(0, kv_count + 7, step, 0)

    def drain(c, _):
        @pl.when(up)
        def _():
            kv_copy(c, 0, 2, 0, me).wait_send()

            @pl.when(me >= 2)
            def _():
                kv_copy(c, 2, 4, 1, me).wait_send()

            @pl.when(me >= 1)
            def _():
                kv_copy(c, 1, 3, 3, me).wait_send()

        @pl.when(jnp.logical_not(odd) | (me >= 3))
        def _():
            kv_copy(c, 0, 1, 2, me).wait_send()

        for slot in range(1, SLOTS):
            @pl.when(me >= slot)
            def _():
                back_copy(c, slot, me).wait_send()
        for what in range(3):
            store(c, what).wait()
        return 0

    lax.fori_loop(0, kv_count, drain, 0)
    for d in range(1, SLOTS):
        @pl.when(me + d < n)
        def _():
            ids_copy(d).wait_send()


def finish(dq_in, dk_in, dv_in, dq_out, dk_out, dv_out, dq_held, dk_held, dv_held, come, go):
    tokens = dq_in.shape[0]
    part = tokens // 4
    moves = [(dq_in, dq_held, dq_out, pl.ds(i * part, part)) for i in range(4)]
    moves.append((dk_in, dk_held, dk_out, pl.ds(0, tokens)))
    moves.append((dv_in, dv_held, dv_out, pl.ds(0, tokens)))
    first = [
        pltpu.make_async_copy(source.at[rows], held.at[rows], come.at[i])
        for i, (source, held, _, rows) in enumerate(moves)
    ]
    second = [
        pltpu.make_async_copy(held.at[rows], target.at[rows], go.at[i])
        for i, (_, held, target, rows) in enumerate(moves)
    ]
    for copy in first:
        copy.start()
    for before, after in zip(first, second):
        before.wait()
        after.start()
    for copy in second:
        copy.wait()


def body(queries, key_heads, value_heads, out_grad, segment_ids):
    tokens, width = queries.shape
    kv_width = key_heads.shape[1]
    kv_count = kv_width // HEAD_DIM
    group = width // kv_width
    n = lax.axis_size("sp")
    assert -(-(MOST - 1) // tokens) == REACH and n % 2 == 0 and group % 2 == 0
    ids_rows = segment_ids.reshape(1, tokens)
    span = SLOTS * tokens
    vmem = pl.BlockSpec(memory_space=pltpu.VMEM)
    pairs = (kv_count, REACH, 2, tokens, HEAD_DIM)
    dma = pltpu.SemaphoreType.DMA
    elements = kv_count * group * tokens * span
    shapes = (
        jax.ShapeDtypeStruct((tokens, width), jnp.bfloat16),
        jax.ShapeDtypeStruct((tokens, kv_width), jnp.bfloat16),
        jax.ShapeDtypeStruct((tokens, kv_width), jnp.bfloat16),
    )
    anywhere = pl.BlockSpec(memory_space=pl.ANY)
    grads = pl.pallas_call(
        functools.partial(kernel, n, kv_count, group),
        out_shape=shapes,
        in_specs=[pl.BlockSpec(memory_space=pltpu.HBM)] * 4 + [vmem],
        out_specs=(anywhere, anywhere, anywhere),
        scratch_shapes=[
            pltpu.VMEM((kv_count, tokens, group * HEAD_DIM), jnp.bfloat16),
            pltpu.VMEM((kv_count, tokens, group * HEAD_DIM), jnp.bfloat16),
            pltpu.VMEM((kv_count, SLOTS, 2, tokens, HEAD_DIM), jnp.bfloat16),
            pltpu.VMEM((SLOTS, 1, tokens), jnp.int32),
            pltpu.VMEM((tokens, tokens), jnp.float32),
            pltpu.VMEM((REACH * tokens, tokens), jnp.float32),
            pltpu.VMEM((REACH * tokens, group * tokens), jnp.float32),
            pltpu.VMEM((REACH * tokens, group * tokens), jnp.float32),
            pltpu.VMEM((span, group * tokens), jnp.bfloat16),
            pltpu.VMEM((span, group * tokens), jnp.bfloat16),
            pltpu.VMEM((kv_count, 3, 2, tokens, HEAD_DIM), jnp.float32),
            pltpu.VMEM(pairs, jnp.bfloat16),
            pltpu.VMEM(pairs, jnp.bfloat16),
            pltpu.VMEM((kv_count, tokens, group * HEAD_DIM), jnp.bfloat16),
            pltpu.VMEM((kv_count, 2, tokens, HEAD_DIM), jnp.bfloat16),
            dma((kv_count, 4)),
            dma((kv_count, 3)),
            dma((kv_count, 4)),
            dma((kv_count, REACH)),
            dma((kv_count, REACH)),
            dma((kv_count, REACH)),
            dma((REACH,)),
            dma((REACH,)),
        ],
        compiler_params=pltpu.CompilerParams(
            collective_id=0, has_side_effects=True, vmem_limit_bytes=61 * 1024 * 1024
        ),
        cost_estimate=pl.CostEstimate(
            flops=10 * elements * HEAD_DIM,
            bytes_accessed=6 * tokens * width + 8 * tokens * kv_width,
            transcendentals=elements,
        ),
    )(queries, key_heads, value_heads, out_grad, ids_rows)
    return pl.pallas_call(
        finish,
        out_shape=shapes,
        in_specs=[anywhere] * 3,
        out_specs=(anywhere, anywhere, anywhere),
        scratch_shapes=[pltpu.VMEM(shape.shape, jnp.bfloat16) for shape in shapes]
        + [dma((6,)), dma((6,))],
        compiler_params=pltpu.CompilerParams(vmem_limit_bytes=61 * 1024 * 1024),
    )(*grads)


def solution(mesh):
    rows = P(("dp", "sp"), None)
    return jax.shard_map(
        body,
        mesh=mesh,
        in_specs=(rows, rows, rows, rows, P(("dp", "sp"))),
        out_specs=(rows, rows, rows),
        check_vma=False,
    )
```
